32 devices in a mesh: blk: 4 (over y, core), fsdp: 8 (over z, x).
Axes of the slice: x: 2, y: 2, z: 4, core: 2. Of those that a mesh axis runs over, the one named last changes fastest.
Arguments:
- img_feat: bfloat16 [2048, 1536], P(('blk', 'fsdp')), may hold values from -200 to 200
- txt_feat: bfloat16 [2048, 1152], P(('blk', 'fsdp')), may hold values from -200 to 200
- partner: int32 [2048], P(('blk', 'fsdp')), may hold values from 0 to 2047, as said below
- projection: bfloat16 [1536, 1152], P('fsdp'), may hold values from -0.4 to 2.9
- img_gain: float32 [1536], replicated, may hold values from 0.25 to 1.75
- txt_gain: float32 [1152], replicated, may hold values from 0.25 to 1.75
- log_scale: float32 [1], replicated, may hold values from 2.7 to 3.1
- logit_bias: float32 [1], replicated, may hold values from -11 to -9
Outputs:
- loss: float32 [1], replicated
- grad_log_scale: float32 [1], replicated
- grad_bias: float32 [1], replicated
- grad_proj: float32 [1536, 1152], P('fsdp')
- grad_img_gain: float32 [1536], replicated
- grad_txt_gain: float32 [1152], replicated
- grad_img_feat: float32 [2048, 1536], P(('blk', 'fsdp'))
- grad_txt_feat: float32 [2048, 1152], P(('blk', 'fsdp'))
The draws below stay inside these ranges and needn't reach their ends.
Inputs may be any that keep to these rules, and one draw needn't show every extreme that they name: Each image's partner lies in the same aligned block of 64 rows, and every text is the partner of exactly one image.
All inputs are finite; a program needn't handle non-finite values.
Results may differ from the reference program's by a relative error of at most 0.0078.
Values may be sent and summed in bfloat16 or wider, within the bound.
A program may use at most 128 MiB of HBM per device.

```python
import math
import jax
import jax.numpy as jnp
from jax import lax

IMG_WIDTH = 1536
EMB = 1152
B_DEV = 64
BATCH = 2048
N_BLK = 4


def pair_order(key):
    block_count = BATCH // B_DEV
    block_keys = jax.random.split(jax.random.fold_in(key, 101), block_count)

    def block_order(block_key):
        return jax.random.permutation(block_key, B_DEV).astype(jnp.int32)
    orders = jax.vmap(block_order)(block_keys)
    offsets = (jnp.arange(block_count, dtype=jnp.int32) * B_DEV)[:, None]
    return (orders + offsets).reshape(BATCH)


def bounded_normal(key, shape):
    return jnp.clip(jax.random.normal(key, shape, jnp.float32), -4.0, 4.0)


def log_spread(key, shape, lower, upper):
    return jnp.exp(jax.random.uniform(key, shape, jnp.float32, math.log(lower), math.log(upper)))


def topic_latent(key, column_top):
    fine_count = max(BATCH // 8, 1)
    broad_count = max(BATCH // 64, 1)
    fine_table = bounded_normal(jax.random.fold_in(key, 102), (fine_count, EMB))
    broad_table = bounded_normal(jax.random.fold_in(key, 103), (broad_count, EMB))
    fine_ids = jax.random.randint(jax.random.fold_in(key, 104), (BATCH,), 0, fine_count)
    broad_ids = jax.random.randint(jax.random.fold_in(key, 105), (BATCH,), 0, broad_count)
    personal = bounded_normal(jax.random.fold_in(key, 106), (BATCH, EMB))
    columns = log_spread(jax.random.fold_in(key, 108), (1, EMB), 1.0, column_top)
    latent = 1.1 * fine_table[fine_ids] + 0.5 * broad_table[broad_ids] + personal
    return (latent, columns)


def draw_partner(key, part):
    return pair_order(key)


def draw_txt_feat(key, part):
    root_key = key
    key = jax.random.fold_in(key, 11)
    column_top = 10.0
    jitter = bounded_normal(jax.random.fold_in(key, 1), (BATCH, EMB))
    row_scale = log_spread(jax.random.fold_in(key, 2), (BATCH, 1), 0.1, 1.0)
    latent, columns = topic_latent(root_key, column_top)
    return ((latent + 0.3 * jitter) * columns * row_scale).astype(jnp.bfloat16)


def draw_img_feat(key, part):
    root_key = key
    key = jax.random.fold_in(key, 12)
    extra_width = IMG_WIDTH - EMB
    column_top = 10.0
    jitter = bounded_normal(jax.random.fold_in(key, 1), (BATCH, EMB))
    spare = bounded_normal(jax.random.fold_in(key, 3), (BATCH, extra_width))
    row_scale = log_spread(jax.random.fold_in(key, 2), (BATCH, 1), 0.1, 1.0)
    spare_columns = log_spread(jax.random.fold_in(key, 4), (1, extra_width), 1.0, column_top)
    latent, columns = topic_latent(root_key, column_top)
    paired_rows = pair_order(root_key)
    aligned = (latent[paired_rows] + 0.4 * jitter) * columns
    whole = jnp.concatenate([aligned, spare * spare_columns], axis=1)
    return (whole * row_scale).astype(jnp.bfloat16)


def draw_projection(key, part):
    key = jax.random.fold_in(key, 13)
    spread = bounded_normal(key, (IMG_WIDTH, EMB))
    anchor = jnp.eye(IMG_WIDTH, EMB, dtype=jnp.float32)
    return (2.5 * anchor + spread / math.sqrt(IMG_WIDTH)).astype(jnp.bfloat16)


def setup_inputs(seed: int = 0) -> dict:
    streams_of = jax.random.split(jax.random.key(seed), 9)
    return {
        "img_feat": draw_img_feat(jax.random.fold_in(streams_of[8], 71), 0),
        "txt_feat": draw_txt_feat(jax.random.fold_in(streams_of[8], 71), 0),
        "partner": draw_partner(jax.random.fold_in(streams_of[8], 71), 0),
        "projection": draw_projection(jax.random.fold_in(streams_of[8], 71), 0),
        "img_gain": jnp.clip(1.0 + 0.15 * jax.random.normal(streams_of[4], (IMG_WIDTH,), jnp.float32), 0.25, 1.75),
        "txt_gain": jnp.clip(1.0 + 0.15 * jax.random.normal(streams_of[5], (EMB,), jnp.float32), 0.25, 1.75),
        "log_scale": jnp.clip(jax.random.uniform(streams_of[6], (1,), jnp.float32, 2.7, 3.1), 2.7, 3.1),
        "logit_bias": jnp.clip(jax.random.uniform(streams_of[7], (1,), jnp.float32, -11.0, -9.0), -11.0, -9.0),
    }


EPSILON = 1e-06

def layer_norm(features):
    values = features.astype(jnp.float32)
    centered = values - lax.optimization_barrier(jnp.mean(values, axis=1, keepdims=True))
    inverse = lax.rsqrt(lax.optimization_barrier(jnp.mean(centered * centered, axis=1, keepdims=True)) + EPSILON)
    return (centered * inverse, inverse)

def layer_norm_back(upstream, normed, inverse, gains):
    scaled = upstream * gains
    return inverse * (scaled - lax.optimization_barrier(jnp.mean(scaled, axis=1, keepdims=True)) - normed * lax.optimization_barrier(jnp.mean(scaled * normed, axis=1, keepdims=True)))

def unit_rows(values):
    length = jnp.sqrt(lax.optimization_barrier(jnp.sum(values * values, axis=1, keepdims=True)) + EPSILON)
    return (values / length, length)

def unit_rows_back(upstream, values, length):
    product = lax.optimization_barrier(jnp.sum(values * upstream, axis=1, keepdims=True))
    return upstream / length - values * product / (length * length * length)

def reference(img_feat, txt_feat, partner, projection, img_gain, txt_gain, log_scale, logit_bias):
    batch_total = img_feat.shape[0]
    temper = jnp.exp(log_scale[0])
    offset = logit_bias[0]
    img_hat, img_inv = layer_norm(img_feat)
    img_norm = (img_hat * img_gain).astype(jnp.bfloat16)
    img_proj = jnp.dot(img_norm, projection, preferred_element_type=jnp.float32)
    img_unit, img_len = unit_rows(img_proj)
    img_emb = img_unit.astype(jnp.bfloat16)
    txt_hat, txt_inv = layer_norm(txt_feat)
    txt_scaled = txt_hat * txt_gain
    txt_unit, txt_len = unit_rows(txt_scaled)
    txt_emb = txt_unit.astype(jnp.bfloat16)
    block_rows = B_DEV * N_BLK
    blocks = batch_total // block_rows
    columns = jnp.arange(batch_total, dtype=jnp.int32)

    def pass_block(running, block_item):
        grad_txt, loss_sum, bias_sum, scale_sum = running
        row_emb, targets = block_item
        similar = jnp.dot(row_emb, txt_emb.T, preferred_element_type=jnp.float32)
        logits = temper * similar + offset
        labels = jnp.where(columns[None, :] == targets[:, None], 1.0, -1.0).astype(jnp.float32)
        margin = labels * logits
        dlogit = -labels * jax.nn.sigmoid(-margin) / batch_total
        weighted = (temper * dlogit).astype(jnp.bfloat16)
        grad_rows = jnp.dot(weighted, txt_emb, preferred_element_type=jnp.float32)
        grad_txt = grad_txt + jnp.dot(weighted.T, row_emb, preferred_element_type=jnp.float32)
        running = (grad_txt, loss_sum + jnp.sum(jax.nn.softplus(-margin)), bias_sum + jnp.sum(dlogit), scale_sum + jnp.sum(dlogit * temper * similar))
        return (running, grad_rows)
    starting = (jnp.zeros((batch_total, EMB), jnp.float32), jnp.zeros((), jnp.float32), jnp.zeros((), jnp.float32), jnp.zeros((), jnp.float32))
    finished, grad_blocks = lax.scan(pass_block, starting, (img_emb.reshape(blocks, block_rows, EMB), partner.astype(jnp.int32).reshape(blocks, block_rows)))
    grad_txt_emb, loss_sum, bias_sum, scale_sum = finished
    grad_img_emb = grad_blocks.reshape(batch_total, EMB)
    grad_img_proj = unit_rows_back(grad_img_emb, img_proj, img_len).astype(jnp.bfloat16)
    grad_proj = jnp.dot(img_norm.T, grad_img_proj, preferred_element_type=jnp.float32)
    grad_img_norm = jnp.dot(grad_img_proj, projection.T, preferred_element_type=jnp.float32)
    grad_img_gain = lax.optimization_barrier(jnp.sum(grad_img_norm * img_hat, axis=0))
    grad_img_feat = layer_norm_back(grad_img_norm, img_hat, img_inv, img_gain)
    grad_txt_scaled = unit_rows_back(grad_txt_emb, txt_scaled, txt_len)
    grad_txt_gain = lax.optimization_barrier(jnp.sum(grad_txt_scaled * txt_hat, axis=0))
    grad_txt_feat = layer_norm_back(grad_txt_scaled, txt_hat, txt_inv, txt_gain)
    return ((loss_sum / batch_total).reshape(1), scale_sum.reshape(1), bias_sum.reshape(1), grad_proj, grad_img_gain, grad_txt_gain, grad_img_feat, grad_txt_feat)
```

```python
import functools

import jax
import jax.numpy as jnp
from jax import lax
from jax.experimental import pallas as pl
from jax.experimental.pallas import tpu as pltpu
from jax.sharding import PartitionSpec as P

EPSILON = 1e-06


def layer_norm(features):
    values = features.astype(jnp.float32)
    centered = values - jnp.mean(values, axis=1, keepdims=True)
    inverse = lax.rsqrt(jnp.mean(centered * centered, axis=1, keepdims=True) + EPSILON)
    return (centered * inverse, inverse)


def layer_norm_back(upstream, normed, inverse, gains):
    scaled = upstream * gains
    return inverse * (
        scaled
        - jnp.mean(scaled, axis=1, keepdims=True)
        - normed * jnp.mean(scaled * normed, axis=1, keepdims=True)
    )


def unit_rows(values):
    length = jnp.sqrt(jnp.sum(values * values, axis=1, keepdims=True) + EPSILON)
    return (values / length, length)


def unit_rows_back(upstream, values, length):
    product = jnp.sum(values * upstream, axis=1, keepdims=True)
    return upstream / length - values * product / (length * length * length)


def pair_terms(img_set, txt_set, targets, temper, offset, batch_total):
    similar = lax.dot_general(
        img_set, txt_set, (((1,), (1,)), ((), ())), preferred_element_type=jnp.float32
    )
    columns = lax.broadcasted_iota(jnp.int32, similar.shape, 1)
    labels = jnp.where(columns == targets[:, None], 1.0, -1.0).astype(jnp.float32)
    margin = labels * (temper * similar + offset)
    dlogit = -labels * jax.nn.sigmoid(-margin) / batch_total
    weighted = (temper * dlogit).astype(jnp.bfloat16)
    partial_sums = (
        jnp.sum(jax.nn.softplus(-margin)),
        jnp.sum(dlogit),
        jnp.sum(dlogit * temper * similar),
    )
    return (weighted, partial_sums)


def shards(img_feat, txt_feat, partner, projection, img_gain, txt_gain, log_scale, logit_bias):
    local_rows = img_feat.shape[0]
    group_count = lax.axis_size("blk")
    member_count = lax.axis_size("fsdp")
    batch_total = local_rows * group_count * member_count
    group_index = lax.axis_index("blk")
    member_index = lax.axis_index("fsdp")
    temper = jnp.exp(log_scale[0])
    offset = logit_bias[0]
    img_hat, img_inv = layer_norm(img_feat)
    img_norm = (img_hat * img_gain).astype(jnp.bfloat16)
    full_proj = lax.all_gather(projection, "fsdp", axis=0, tiled=True)
    img_proj = jnp.dot(img_norm, full_proj, preferred_element_type=jnp.float32)
    img_unit, img_len = unit_rows(img_proj)
    img_emb = img_unit.astype(jnp.bfloat16)
    txt_hat, txt_inv = layer_norm(txt_feat)
    txt_scaled = txt_hat * txt_gain
    txt_unit, txt_len = unit_rows(txt_scaled)
    txt_emb = txt_unit.astype(jnp.bfloat16)
    own_offsets = partner - (group_index * member_count + member_index) * local_rows
    txt_set = lax.all_gather(txt_emb, "fsdp", axis=0, tiled=True)
    block_targets = own_offsets + member_index * local_rows
    block_rows = img_emb.shape[0]
    set_rows = group_count * block_rows
    img_set = lax.all_gather(img_emb, "blk", axis=0, tiled=True)
    targets = jnp.full((set_rows,), -1, jnp.int32)
    targets = lax.dynamic_update_slice(targets, block_targets, (group_index * block_rows,))
    weighted, partial_sums = pair_terms(img_set, txt_set, targets, temper, offset, batch_total)
    grad_block = lax.psum_scatter(
        jnp.dot(weighted, txt_set, preferred_element_type=jnp.float32),
        "blk",
        scatter_dimension=0,
        tiled=True,
    )
    grad_txt_emb = lax.psum_scatter(
        lax.dot_general(
            weighted, img_set, (((0,), (0,)), ((), ())), preferred_element_type=jnp.float32
        ),
        "fsdp",
        scatter_dimension=0,
        tiled=True,
    )
    grad_img_proj = unit_rows_back(grad_block, img_proj, img_len).astype(jnp.bfloat16)
    grad_proj = lax.psum_scatter(
        lax.dot_general(
            img_norm, grad_img_proj, (((0,), (0,)), ((), ())), preferred_element_type=jnp.float32
        ),
        "fsdp",
        scatter_dimension=0,
        tiled=True,
    )
    grad_proj = lax.psum(grad_proj, "blk")
    grad_img_norm = lax.dot_general(
        grad_img_proj, full_proj, (((1,), (1,)), ((), ())), preferred_element_type=jnp.float32
    )
    grad_img_feat = layer_norm_back(grad_img_norm, img_hat, img_inv, img_gain)
    grad_txt_scaled = unit_rows_back(grad_txt_emb, txt_scaled, txt_len)
    grad_txt_feat = layer_norm_back(grad_txt_scaled, txt_hat, txt_inv, txt_gain)
    totals = lax.psum(
        (
            partial_sums[0],
            partial_sums[1],
            partial_sums[2],
            jnp.sum(grad_img_norm * img_hat, axis=0),
            jnp.sum(grad_txt_scaled * txt_hat, axis=0),
        ),
        ("blk", "fsdp"),
    )
    return (
        (totals[0] / batch_total).reshape(1),
        totals[2].reshape(1),
        totals[1].reshape(1),
        grad_proj,
        totals[3],
        totals[4],
        grad_img_feat,
        grad_txt_feat,
    )


MESH = pl.DeviceIdType.MESH
BF16 = jnp.bfloat16
F32 = jnp.float32


def txt_slot(distance):
    return distance // 2 if distance % 2 else 4 + distance // 2


def flip(bit, yes):
    return 1 - bit if yes else bit


def matmul(left, right):
    return jnp.dot(left, right, preferred_element_type=F32)


def matmul_nt(left, right):
    return lax.dot_general(left, right, (((1,), (1,)), ((), ())), preferred_element_type=F32)


def pair_math(similar, labels, temper, offset, batch_total):
    margin = labels * (temper * similar + offset)
    small = jnp.exp(-jnp.abs(margin))
    chance = jnp.where(margin >= 0.0, small, 1.0) / (1.0 + small)
    dlogit = -labels * chance / batch_total
    softplus = jnp.maximum(-margin, 0.0) + jnp.log1p(small)
    return dlogit, softplus


def total(values):
    return jnp.sum(jnp.sum(values, axis=0, keepdims=True), axis=1, keepdims=True)


def kernel(
    batch_total, img_ref, txt_ref, goal_ref, part_ref, igain_ref, tgain_ref, scale_ref, bias_ref,
    loss_ref, gscale_ref, gbias_ref, gproj_ref, gig_ref, gtg_ref, gif_ref, gtf_ref,
    full_ref, norm_ref, hat_ref, turned_ref, turned_in, proj_ref,
    txt_set, img_set, weight_ref, turnw_ref, block_ref, block_out, block_in,
    gtx_ref, gtx_out, gtx_in, gtz_out, gtz_in, grad_set,
    gp_in, gp_out, gp_far, gp_sum, gp_end, small_ref, small_in, mid_ref, mid_in, send_sem, recv_sem,
):
    rows = img_ref.shape[0]
    depth = part_ref.shape[0]
    quarter = depth // 4
    half = depth // 2
    b = lax.axis_index("blk")
    f = lax.axis_index("fsdp")
    core, y = b % 2, b // 2
    x, z_low, z_high = f % 2, (f // 2) % 2, f // 4

    def member(r):
        return (flip(z_high, r & 4) * 2 + flip(z_low, r & 2)) * 2 + flip(x, r & 1)

    def group(r):
        return flip(y, r & 2) * 2 + flip(core, r & 1)

    barrier = pltpu.get_barrier_semaphore()
    for r in range(1, 8):
        pl.semaphore_signal(barrier, inc=1, device_id=(b, member(r)), device_id_type=MESH)
    for r in range(1, 4):
        pl.semaphore_signal(barrier, inc=1, device_id=(group(r), f), device_id_type=MESH)
    pl.semaphore_wait(barrier, 10)

    copies = []

    def send(source, target, to):
        k = len(copies)
        copy = pltpu.make_async_remote_copy(
            src_ref=source, dst_ref=target, send_sem=send_sem.at[k], recv_sem=recv_sem.at[k],
            device_id=to, device_id_type=MESH,
        )
        copy.start()
        copies.append(copy)
        return copy

    def along(r):
        return (b, member(r))

    def across(r):
        return (group(r), f)

    def piece(r, q):
        start = member(r) * depth + group(q) * quarter
        return full_ref.at[pl.ds(pl.multiple_of(start, 16), quarter), :]

    own_piece = part_ref.at[pl.ds(pl.multiple_of(b * quarter, 16), quarter), :]
    arrive = {}
    for r in (4, 6, 2, 1):
        arrive[r, 0] = send(own_piece, piece(0, 0), along(r))
    full_ref[pl.ds(pl.multiple_of(f * depth, 16), depth), :] = part_ref[...]

    values = txt_ref[...].astype(F32)
    centered = values - jnp.mean(values, axis=1, keepdims=True)
    txt_inv = lax.rsqrt(jnp.mean(centered * centered, axis=1, keepdims=True) + EPSILON)
    txt_hat = centered * txt_inv
    txt_scaled = txt_hat * tgain_ref[...]
    txt_len = jnp.sqrt(jnp.sum(txt_scaled * txt_scaled, axis=1, keepdims=True) + EPSILON)
    txt_set[txt_slot(0)] = (txt_scaled / txt_len).astype(BF16)
    txt_arrive = {}
    for r in (4, 6, 2, 1):
        txt_arrive[r] = send(txt_set.at[txt_slot(0)], txt_set.at[txt_slot(r)], along(r))

    values = img_ref[...].astype(F32)
    centered = values - jnp.mean(values, axis=1, keepdims=True)
    img_inv = lax.rsqrt(jnp.mean(centered * centered, axis=1, keepdims=True) + EPSILON)
    img_hat = centered * img_inv
    hat_ref[...] = img_hat
    img_norm = img_hat * igain_ref[...]
    norm_ref[...] = img_norm.astype(BF16)
    turned_ref[...] = jnp.transpose(img_norm).astype(BF16)

    for r in (2, 4, 6):
        arrive[r, 0].wait_recv()
        arrive[r + 1, 0] = send(piece(r, 0), piece(r, 0), along(1))
        arrive[r, 2] = send(piece(r, 0), piece(r, 0), across(2))
        arrive[r, 1] = send(piece(r, 0), piece(r, 0), across(1))
    for r in (1, 3, 5, 7):
        arrive[r, 0].wait_recv()
        arrive[r, 2] = send(piece(r, 0), piece(r, 0), across(2))
        arrive[r, 1] = send(piece(r, 0), piece(r, 0), across(1))
    for r in (2, 4, 6):
        txt_arrive[r].wait_recv()
        txt_arrive[r + 1] = send(
            txt_set.at[txt_slot(r)], txt_set.at[txt_slot(r + 1)], along(1)
        )
    for r in (2, 4, 6, 1, 3, 5, 7):
        arrive[r, 2].wait_recv()
        arrive[r, 3] = send(piece(r, 2), piece(r, 2), across(1))
    img_proj = None
    for r in (0, 2, 4, 6):
        for s in (r, r + 1):
            if s:
                arrive[s, 1].wait_recv()
                arrive[s, 3].wait_recv()
        pair = member(r) // 2 * (2 * depth)
        pair = pl.ds(pl.multiple_of(pair, 128), 2 * depth)
        term = matmul(norm_ref[:, pair], full_ref[pair, :])
        img_proj = term if img_proj is None else img_proj + term
    proj_ref[...] = img_proj
    img_len = jnp.sqrt(jnp.sum(img_proj * img_proj, axis=1, keepdims=True) + EPSILON)
    img_set[0:rows] = (img_proj / img_len).astype(BF16)
    own = img_set.at[0:rows]
    from_y = send(own, img_set.at[2 * rows:3 * rows], across(2))
    from_core = send(own, img_set.at[rows:2 * rows], across(1))
    turned_arrive = {}
    for r in (2, 4, 6, 1, 3, 5, 7):
        rows_of = pl.ds(pl.multiple_of(member(r) * depth, 16), depth)
        turned_arrive[r] = send(turned_ref.at[rows_of, :], turned_in.at[r], along(r))
    turned_in[0] = turned_ref[pl.ds(pl.multiple_of(f * depth, 16), depth), :]

    for r in (1, 3, 5, 7):
        txt_arrive[r].wait_recv()
    txt_all = txt_set[...].reshape(8 * rows, txt_set.shape[2])
    temper = jnp.exp(scale_ref[...])
    offset = bias_ref[...]
    similar = matmul_nt(img_set[0:rows], txt_all)
    columns = lax.broadcasted_iota(jnp.int32, similar.shape, 1)
    goal = goal_ref[...] - (b * 8 + f) * rows + txt_slot(0) * rows
    labels = jnp.where(columns == goal, 1.0, -1.0).astype(F32)
    dlogit, softplus = pair_math(similar, labels, temper, offset, batch_total)
    weighted = temper * dlogit
    weight_ref[0:rows] = weighted.astype(BF16)
    turnw_ref[:, 0:rows] = jnp.transpose(weighted).astype(BF16)
    loss = total(softplus)
    grad_bias = total(dlogit)
    grad_scale = total(weighted * similar)
    from_y.wait_recv()
    from_far = send(img_set.at[2 * rows:3 * rows], img_set.at[3 * rows:4 * rows], across(1))
    from_core.wait_recv()
    from_far.wait_recv()
    similar = matmul_nt(img_set[rows:4 * rows], txt_all)
    dlogit, softplus = pair_math(similar, -1.0, temper, offset, batch_total)
    weighted = temper * dlogit
    weight_ref[rows:4 * rows] = weighted.astype(BF16)
    block = matmul(weight_ref[...], txt_all)
    block_out[0] = block[rows:2 * rows].astype(BF16)
    block_out[1] = block[3 * rows:4 * rows].astype(BF16)
    near = send(block_out.at[0], block_in.at[0], across(1))
    far = send(block_out.at[1], block_in.at[1], across(1))
    block_ref[0] = block[0:rows]
    block_ref[1] = block[2 * rows:3 * rows]
    turnw_ref[:, rows:4 * rows] = jnp.transpose(weighted).astype(BF16)
    loss = loss + total(softplus)
    grad_bias = grad_bias + total(dlogit)
    grad_scale = grad_scale + total(weighted * similar)
    far.wait_recv()
    block_out[2] = (block_ref[1] + block_in[1].astype(F32)).astype(BF16)
    wide = send(block_out.at[2], block_in.at[2], across(2))

    odd = matmul(turnw_ref[0:4 * rows], img_set[...]).astype(BF16)
    gtx_out[...] = odd.reshape(gtx_out.shape)
    gtx_arrive = [
        send(gtx_out.at[k], gtx_in.at[k], along(1)) for k in (1, 2, 3, 0)
    ]
    gtx_ref[...] = matmul(turnw_ref[4 * rows:8 * rows], img_set[...]).reshape(gtx_ref.shape)

    near.wait_recv()
    wide.wait_recv()
    img_proj = proj_ref[...]
    grad = block_ref[0] + block_in[0].astype(F32) + block_in[2].astype(F32)
    product = jnp.sum(img_proj * grad, axis=1, keepdims=True)
    grad = grad / img_len - img_proj * product / (img_len * img_len * img_len)
    grad_set[0] = grad.astype(BF16)
    grad_arrive = {}
    for r in (4, 6, 2, 1):
        grad_arrive[r] = send(grad_set.at[0], grad_set.at[r], along(r))

    gtz_arrive = {}
    for k in (1, 2, 3):
        gtx_arrive[k - 1].wait_recv()
        gtz_out[k] = (gtx_ref[k] + gtx_in[k].astype(F32)).astype(BF16)
        gtz_arrive[k] = send(gtz_out.at[k], gtz_in.at[k], along(2 * k))

    grad_norm = matmul_nt(grad_set[0], full_ref[...])
    img_hat = hat_ref[...]
    img_gain_sum = jnp.sum(grad_norm * img_hat, axis=0, keepdims=True)
    scaled = grad_norm * igain_ref[...]
    gif_ref[...] = img_inv * (
        scaled
        - jnp.mean(scaled, axis=1, keepdims=True)
        - img_hat * jnp.mean(scaled * img_hat, axis=1, keepdims=True)
    )

    for r in (2, 4, 6):
        grad_arrive[r].wait_recv()
        grad_arrive[r + 1] = send(grad_set.at[r], grad_set.at[r + 1], along(1))

    grad_proj = matmul(turned_in[0], grad_set[0])
    for r in (2, 4, 6):
        turned_arrive[r].wait_recv()
        grad_proj = grad_proj + matmul(turned_in[r], grad_set[r])

    gtx_arrive[3].wait_recv()
    grad = gtx_ref[0] + gtx_in[0].astype(F32)
    for k in (1, 2, 3):
        gtz_arrive[k].wait_recv()
        grad = grad + gtz_in[k].astype(F32)
    product = jnp.sum(txt_scaled * grad, axis=1, keepdims=True)
    grad = grad / txt_len - txt_scaled * product / (txt_len * txt_len * txt_len)
    txt_gain_sum = jnp.sum(grad * txt_hat, axis=0, keepdims=True)
    img_tiles = img_ref.shape[1] // 128
    txt_tiles = txt_ref.shape[1] // 128
    small_ref[...] = jnp.zeros_like(small_ref)
    for k in range(img_tiles):
        small_ref[k:k + 1, :] = img_gain_sum[:, k * 128:(k + 1) * 128]
    for k in range(txt_tiles):
        at = img_tiles + k
        small_ref[at:at + 1, :] = txt_gain_sum[:, k * 128:(k + 1) * 128]
    at = img_tiles + txt_tiles
    lanes = lax.broadcasted_iota(jnp.int32, (1, 128), 1)
    small_ref[at:at + 1, :] = jnp.where(
        lanes == 0, loss, jnp.where(lanes == 1, grad_scale, jnp.where(lanes == 2, grad_bias, 0.0))
    )
    small_arrive = [send(small_ref, small_in.at[b], across(r)) for r in (1, 2, 3)]

    scaled = grad * tgain_ref[...]
    gtf_ref[...] = txt_inv * (
        scaled
        - jnp.mean(scaled, axis=1, keepdims=True)
        - txt_hat * jnp.mean(scaled * txt_hat, axis=1, keepdims=True)
    )

    for r in (1, 3, 5, 7):
        turned_arrive[r].wait_recv()
        grad_arrive[r].wait_recv()
        grad_proj = grad_proj + matmul(turned_in[r], grad_set[r])
    gproj_ref[...] = grad_proj
    mine = pl.ds(pl.multiple_of(core * half, 16), half)
    other = pl.ds(pl.multiple_of((1 - core) * half, 16), half)
    gp_first = send(gproj_ref.at[other, :], gp_in, across(1))

    small_in[b] = small_ref[...]
    for copy in small_arrive:
        copy.wait_recv()
    mid_ref[...] = (small_in[0] + small_in[1]) + (small_in[2] + small_in[3])
    mid_arrive = [send(mid_ref, mid_in.at[f], along(r)) for r in range(1, 8)]
    mid_in[f] = mid_ref[...]

    gp_first.wait()
    gp_out[...] = (gproj_ref[mine, :] + gp_in[...]).astype(BF16)
    gp_step = send(gp_out, gp_far, across(2))

    for copy in mid_arrive:
        copy.wait_recv()
    sums = mid_in[0]
    for k in range(1, 8):
        sums = sums + mid_in[k]
    for k in range(img_tiles):
        gig_ref[:, k * 128:(k + 1) * 128] = sums[k:k + 1, :]
    for k in range(txt_tiles):
        at = img_tiles + k
        gtg_ref[:, k * 128:(k + 1) * 128] = sums[at:at + 1, :]
    at = img_tiles + txt_tiles
    loss_ref[...] = sums[at:at + 1, 0:1] / batch_total
    gscale_ref[...] = sums[at:at + 1, 1:2]
    gbias_ref[...] = sums[at:at + 1, 2:3]

    gp_step.wait_recv()
    gp_sum[...] = gp_out[...].astype(F32) + gp_far[...].astype(F32)
    gp_last = send(gp_sum, gp_end, across(1))
    gproj_ref[mine, :] = gp_sum[...]
    gp_last.wait_recv()
    gproj_ref[other, :] = gp_end[...]

    for copy in copies:
        if copy is not gp_first:
            copy.wait_send()


def fused_shards(img_feat, txt_feat, partner, projection, img_gain, txt_gain, log_scale, logit_bias):
    rows, width = img_feat.shape
    emb = txt_feat.shape[1]
    depth = projection.shape[0]
    batch_total = rows * lax.axis_size("blk") * lax.axis_size("fsdp")
    small_rows = -(-((width + emb) // 128 + 1) // 8) * 8
    scalar = jax.ShapeDtypeStruct((1, 1), F32)
    vmem = pltpu.VMEM
    outs = pl.pallas_call(
        functools.partial(kernel, batch_total),
        out_shape=(
            scalar,
            scalar,
            scalar,
            jax.ShapeDtypeStruct((depth, emb), F32),
            jax.ShapeDtypeStruct((1, width), F32),
            jax.ShapeDtypeStruct((1, emb), F32),
            jax.ShapeDtypeStruct((rows, width), F32),
            jax.ShapeDtypeStruct((rows, emb), F32),
        ),
        in_specs=[pl.BlockSpec(memory_space=vmem)] * 8,
        out_specs=tuple([pl.BlockSpec(memory_space=vmem)] * 8),
        scratch_shapes=[
            vmem((width, emb), BF16),
            vmem((rows, width), BF16),
            vmem((rows, width), F32),
            vmem((width, rows), BF16),
            vmem((8, depth, rows), BF16),
            vmem((rows, emb), F32),
            vmem((8, rows, emb), BF16),
            vmem((4 * rows, emb), BF16),
            vmem((4 * rows, 8 * rows), BF16),
            vmem((8 * rows, 4 * rows), BF16),
            vmem((2, rows, emb), F32),
            vmem((3, rows, emb), BF16),
            vmem((3, rows, emb), BF16),
            vmem((4, rows, emb), F32),
            vmem((4, rows, emb), BF16),
            vmem((4, rows, emb), BF16),
            vmem((4, rows, emb), BF16),
            vmem((4, rows, emb), BF16),
            vmem((8, rows, emb), BF16),
            vmem((depth // 2, emb), F32),
            vmem((depth // 2, emb), BF16),
            vmem((depth // 2, emb), BF16),
            vmem((depth // 2, emb), F32),
            vmem((depth // 2, emb), F32),
            vmem((small_rows, 128), F32),
            vmem((4, small_rows, 128), F32),
            vmem((small_rows, 128), F32),
            vmem((8, small_rows, 128), F32),
            pltpu.SemaphoreType.DMA((80,)),
            pltpu.SemaphoreType.DMA((80,)),
        ],
        compiler_params=pltpu.CompilerParams(
            collective_id=0, has_side_effects=True, vmem_limit_bytes=48 * 1024 * 1024
        ),
    )(
        img_feat,
        txt_feat,
        partner.reshape(rows, 1),
        projection,
        img_gain.reshape(1, width),
        txt_gain.reshape(1, emb),
        log_scale.reshape(1, 1),
        logit_bias.reshape(1, 1),
    )
    loss, grad_scale, grad_bias, grad_proj, img_sum, txt_sum, img_grad, txt_grad = outs
    return (
        loss.reshape(1),
        grad_scale.reshape(1),
        grad_bias.reshape(1),
        grad_proj,
        img_sum.reshape(width),
        txt_sum.reshape(emb),
        img_grad,
        txt_grad,
    )


def solution(mesh):
    placed = (
        P(("blk", "fsdp"), None),
        P(("blk", "fsdp"), None),
        P(("blk", "fsdp")),
        P("fsdp", None),
        P(),
        P(),
        P(),
        P(),
    )
    fused = mesh.shape["blk"] == 4 and mesh.shape["fsdp"] == 8
    return jax.shard_map(
        fused_shards if fused else shards,
        mesh=mesh,
        in_specs=placed,
        out_specs=(
            P(),
            P(),
            P(),
            P("fsdp", None),
            P(),
            P(),
            P(("blk", "fsdp"), None),
            P(("blk", "fsdp"), None),
        ),
        check_vma=False,
    )
```

```python
import functools

import jax
import jax.numpy as jnp
from jax import lax
from jax.experimental import pallas as pl
from jax.experimental.pallas import tpu as pltpu
from jax.sharding import PartitionSpec as P

EPSILON = 1e-06


def layer_norm(features):
    values = features.astype(jnp.float32)
    centered = values - jnp.mean(values, axis=1, keepdims=True)
    inverse = lax.rsqrt(jnp.mean(centered * centered, axis=1, keepdims=True) + EPSILON)
    return (centered * inverse, inverse)


def layer_norm_back(upstream, normed, inverse, gains):
    scaled = upstream * gains
    return inverse * (
        scaled
        - jnp.mean(scaled, axis=1, keepdims=True)
        - normed * jnp.mean(scaled * normed, axis=1, keepdims=True)
    )


def unit_rows(values):
    length = jnp.sqrt(jnp.sum(values * values, axis=1, keepdims=True) + EPSILON)
    return (values / length, length)


def unit_rows_back(upstream, values, length):
    product = jnp.sum(values * upstream, axis=1, keepdims=True)
    return upstream / length - values * product / (length * length * length)


def pair_terms(img_set, txt_set, targets, temper, offset, batch_total):
    similar = lax.dot_general(
        img_set, txt_set, (((1,), (1,)), ((), ())), preferred_element_type=jnp.float32
    )
    columns = lax.broadcasted_iota(jnp.int32, similar.shape, 1)
    labels = jnp.where(columns == targets[:, None], 1.0, -1.0).astype(jnp.float32)
    margin = labels * (temper * similar + offset)
    dlogit = -labels * jax.nn.sigmoid(-margin) / batch_total
    weighted = (temper * dlogit).astype(jnp.bfloat16)
    partial_sums = (
        jnp.sum(jax.nn.softplus(-margin)),
        jnp.sum(dlogit),
        jnp.sum(dlogit * temper * similar),
    )
    return (weighted, partial_sums)


def shards(img_feat, txt_feat, partner, projection, img_gain, txt_gain, log_scale, logit_bias):
    local_rows = img_feat.shape[0]
    group_count = lax.axis_size("blk")
    member_count = lax.axis_size("fsdp")
    batch_total = local_rows * group_count * member_count
    group_index = lax.axis_index("blk")
    member_index = lax.axis_index("fsdp")
    temper = jnp.exp(log_scale[0])
    offset = logit_bias[0]
    img_hat, img_inv = layer_norm(img_feat)
    img_norm = (img_hat * img_gain).astype(jnp.bfloat16)
    full_proj = lax.all_gather(projection, "fsdp", axis=0, tiled=True)
    img_proj = jnp.dot(img_norm, full_proj, preferred_element_type=jnp.float32)
    img_unit, img_len = unit_rows(img_proj)
    img_emb = img_unit.astype(jnp.bfloat16)
    txt_hat, txt_inv = layer_norm(txt_feat)
    txt_scaled = txt_hat * txt_gain
    txt_unit, txt_len = unit_rows(txt_scaled)
    txt_emb = txt_unit.astype(jnp.bfloat16)
    own_offsets = partner - (group_index * member_count + member_index) * local_rows
    txt_set = lax.all_gather(txt_emb, "fsdp", axis=0, tiled=True)
    block_targets = own_offsets + member_index * local_rows
    block_rows = img_emb.shape[0]
    set_rows = group_count * block_rows
    img_set = lax.all_gather(img_emb, "blk", axis=0, tiled=True)
    targets = jnp.full((set_rows,), -1, jnp.int32)
    targets = lax.dynamic_update_slice(targets, block_targets, (group_index * block_rows,))
    weighted, partial_sums = pair_terms(img_set, txt_set, targets, temper, offset, batch_total)
    grad_block = lax.psum_scatter(
        jnp.dot(weighted, txt_set, preferred_element_type=jnp.float32),
        "blk",
        scatter_dimension=0,
        tiled=True,
    )
    grad_txt_emb = lax.psum_scatter(
        lax.dot_general(
            weighted, img_set, (((0,), (0,)), ((), ())), preferred_element_type=jnp.float32
        ),
        "fsdp",
        scatter_dimension=0,
        tiled=True,
    )
    grad_img_proj = unit_rows_back(grad_block, img_proj, img_len).astype(jnp.bfloat16)
    grad_proj = lax.psum_scatter(
        lax.dot_general(
            img_norm, grad_img_proj, (((0,), (0,)), ((), ())), preferred_element_type=jnp.float32
        ),
        "fsdp",
        scatter_dimension=0,
        tiled=True,
    )
    grad_proj = lax.psum(grad_proj, "blk")
    grad_img_norm = lax.dot_general(
        grad_img_proj, full_proj, (((1,), (1,)), ((), ())), preferred_element_type=jnp.float32
    )
    grad_img_feat = layer_norm_back(grad_img_norm, img_hat, img_inv, img_gain)
    grad_txt_scaled = unit_rows_back(grad_txt_emb, txt_scaled, txt_len)
    grad_txt_feat = layer_norm_back(grad_txt_scaled, txt_hat, txt_inv, txt_gain)
    totals = lax.psum(
        (
            partial_sums[0],
            partial_sums[1],
            partial_sums[2],
            jnp.sum(grad_img_norm * img_hat, axis=0),
            jnp.sum(grad_txt_scaled * txt_hat, axis=0),
        ),
        ("blk", "fsdp"),
    )
    return (
        (totals[0] / batch_total).reshape(1),
        totals[2].reshape(1),
        totals[1].reshape(1),
        grad_proj,
        totals[3],
        totals[4],
        grad_img_feat,
        grad_txt_feat,
    )


MESH = pl.DeviceIdType.MESH
BF16 = jnp.bfloat16
F32 = jnp.float32


def txt_slot(distance):
    return distance // 2 if distance % 2 else 4 + distance // 2


def flip(bit, yes):
    return 1 - bit if yes else bit


def matmul(left, right):
    return jnp.dot(left, right, preferred_element_type=F32)


def matmul_nt(left, right):
    return lax.dot_general(left, right, (((1,), (1,)), ((), ())), preferred_element_type=F32)


def pair_math(similar, labels, temper, offset, batch_total):
    margin = labels * (temper * similar + offset)
    small = jnp.exp(-jnp.abs(margin))
    chance = jnp.where(margin >= 0.0, small, 1.0) / (1.0 + small)
    dlogit = -labels * chance / batch_total
    softplus = jnp.maximum(-margin, 0.0) + jnp.log1p(small)
    return dlogit, softplus


def total(values):
    return jnp.sum(jnp.sum(values, axis=0, keepdims=True), axis=1, keepdims=True)


def kernel(
    batch_total, img_hbm, txt_hbm, goal_ref, part_ref, igain_hbm, tgain_hbm, scale_ref, bias_ref,
    loss_ref, gscale_ref, gbias_ref, gproj_ref, gig_ref, gtg_ref, gif_ref, gtf_ref,
    img_ref, txt_ref, igain_ref, tgain_ref, full_ref, norm_ref, hat_ref, turned_ref, turned_in, proj_ref,
    txt_set, img_set, weight_ref, turnw_ref, block_ref, block_out, block_in,
    gtx_ref, gtx_out, gtx_in, gtz_out, gtz_in, grad_set,
    gp_in, gp_out, gp_far, gp_sum, gp_end, small_ref, small_in, mid_ref, mid_in, back_ref,
    load_sem, send_sem, recv_sem,
):
    rows = img_ref.shape[0]
    depth = part_ref.shape[0]
    quarter = depth // 4
    half = depth // 2
    b = lax.axis_index("blk")
    f = lax.axis_index("fsdp")
    core, y = b % 2, b // 2
    x, z_low, z_high = f % 2, (f // 2) % 2, f // 4

    def member(r):
        return (flip(z_high, r & 4) * 2 + flip(z_low, r & 2)) * 2 + flip(x, r & 1)

    def group(r):
        return flip(y, r & 2) * 2 + flip(core, r & 1)

    own_rows = full_ref.at[pl.ds(pl.multiple_of(f * depth, 16), depth), :]
    loads = []
    for source, target in (
        (txt_hbm, txt_ref), (tgain_hbm, tgain_ref), (img_hbm, img_ref), (igain_hbm, igain_ref),
        (part_ref, own_rows),
    ):
        loads.append(pltpu.make_async_copy(source, target, load_sem.at[len(loads)]))
        loads[-1].start()

    barrier = pltpu.get_barrier_semaphore()
    for r in range(1, 8):
        pl.semaphore_signal(barrier, inc=1, device_id=(b, member(r)), device_id_type=MESH)
    for r in range(1, 4):
        pl.semaphore_signal(barrier, inc=1, device_id=(group(r), f), device_id_type=MESH)
    pl.semaphore_wait(barrier, 10)

    copies = []

    def send(source, target, to):
        k = len(copies)
        copy = pltpu.make_async_remote_copy(
            src_ref=source, dst_ref=target, send_sem=send_sem.at[k], recv_sem=recv_sem.at[k],
            device_id=to, device_id_type=MESH,
        )
        copy.start()
        copies.append(copy)
        return copy

    def along(r):
        return (b, member(r))

    def across(r):
        return (group(r), f)

    def piece(r, q):
        start = member(r) * depth + group(q) * quarter
        return full_ref.at[pl.ds(pl.multiple_of(start, 16), quarter), :]

    own_piece = part_ref.at[pl.ds(pl.multiple_of(b * quarter, 16), quarter), :]
    arrive = {}
    for r in (4, 6, 2, 1):
        arrive[r, 0] = send(own_piece, piece(0, 0), along(r))

    loads[0].wait()
    loads[1].wait()
    values = txt_ref[...].astype(F32)
    centered = values - jnp.mean(values, axis=1, keepdims=True)
    txt_inv = lax.rsqrt(jnp.mean(centered * centered, axis=1, keepdims=True) + EPSILON)
    txt_hat = centered * txt_inv
    txt_scaled = txt_hat * tgain_ref[...]
    txt_len = jnp.sqrt(jnp.sum(txt_scaled * txt_scaled, axis=1, keepdims=True) + EPSILON)
    txt_set[txt_slot(0)] = (txt_scaled / txt_len).astype(BF16)
    txt_arrive = {}
    for r in (4, 6, 2, 1):
        txt_arrive[r] = send(txt_set.at[txt_slot(0)], txt_set.at[txt_slot(r)], along(r))

    def spread(r):
        arrive[r, 0].wait_recv()
        if r % 2 == 0:
            arrive[r + 1, 0] = send(piece(r, 0), piece(r, 0), along(1))
        arrive[r, 2] = send(piece(r, 0), piece(r, 0), across(2))
        arrive[r, 1] = send(piece(r, 0), piece(r, 0), across(1))

    spread(2)

    loads[2].wait()
    loads[3].wait()
    values = img_ref[...].astype(F32)
    centered = values - jnp.mean(values, axis=1, keepdims=True)
    img_inv = lax.rsqrt(jnp.mean(centered * centered, axis=1, keepdims=True) + EPSILON)
    img_hat = centered * img_inv
    hat_ref[...] = img_hat
    img_norm = img_hat * igain_ref[...]
    norm_ref[...] = img_norm.astype(BF16)
    for r in (4, 6):
        spread(r)
    turned_ref[...] = jnp.transpose(hat_ref[...] * igain_ref[...]).astype(BF16)
    for r in (1, 3, 5, 7):
        spread(r)
    for r in (2, 4, 6):
        txt_arrive[r].wait_recv()
        txt_arrive[r + 1] = send(
            txt_set.at[txt_slot(r)], txt_set.at[txt_slot(r + 1)], along(1)
        )
    for r in (2, 4, 6, 1, 3, 5, 7):
        arrive[r, 2].wait_recv()
        arrive[r, 3] = send(piece(r, 2), piece(r, 2), across(1))
    loads[4].wait()
    img_proj = None
    for r in (0, 2, 4, 6):
        for s in (r, r + 1):
            if s:
                arrive[s, 1].wait_recv()
                arrive[s, 3].wait_recv()
        pair = member(r) // 2 * (2 * depth)
        pair = pl.ds(pl.multiple_of(pair, 128), 2 * depth)
        term = matmul(norm_ref[:, pair], full_ref[pair, :])
        img_proj = term if img_proj is None else img_proj + term
    proj_ref[...] = img_proj
    img_len = jnp.sqrt(jnp.sum(img_proj * img_proj, axis=1, keepdims=True) + EPSILON)
    img_set[0:rows] = (img_proj / img_len).astype(BF16)
    own = img_set.at[0:rows]
    from_y = send(own, img_set.at[2 * rows:3 * rows], across(2))
    from_core = send(own, img_set.at[rows:2 * rows], across(1))
    turned_arrive = {}
    for r in (2, 4, 6, 1, 3, 5, 7):
        rows_of = pl.ds(pl.multiple_of(member(r) * depth, 16), depth)
        turned_arrive[r] = send(turned_ref.at[rows_of, :], turned_in.at[r], along(r))
    turned_in[0] = turned_ref[pl.ds(pl.multiple_of(f * depth, 16), depth), :]

    for r in (1, 3, 5, 7):
        txt_arrive[r].wait_recv()
    txt_all = txt_set[...].reshape(8 * rows, txt_set.shape[2])
    temper = jnp.exp(scale_ref[...])
    offset = bias_ref[...]
    similar = matmul_nt(img_set[0:rows], txt_all)
    columns = lax.broadcasted_iota(jnp.int32, similar.shape, 1)
    goal = goal_ref[...] - (b * 8 + f) * rows + txt_slot(0) * rows
    labels = jnp.where(columns == goal, 1.0, -1.0).astype(F32)
    dlogit, softplus = pair_math(similar, labels, temper, offset, batch_total)
    weighted = temper * dlogit
    weight_ref[0:rows] = weighted.astype(BF16)
    turnw_ref[:, 0:rows] = jnp.transpose(weighted).astype(BF16)
    loss = total(softplus)
    grad_bias = total(dlogit)
    grad_scale = total(weighted * similar)
    from_y.wait_recv()
    from_far = send(img_set.at[2 * rows:3 * rows], img_set.at[3 * rows:4 * rows], across(1))
    from_core.wait_recv()
    from_far.wait_recv()
    similar = matmul_nt(img_set[rows:4 * rows], txt_all)
    dlogit, softplus = pair_math(similar, -1.0, temper, offset, batch_total)
    weighted = temper * dlogit
    weight_ref[rows:4 * rows] = weighted.astype(BF16)
    block = matmul(weight_ref[...], txt_all)
    block_out[0] = block[rows:2 * rows].astype(BF16)
    block_out[1] = block[3 * rows:4 * rows].astype(BF16)
    near = send(block_out.at[0], block_in.at[0], across(1))
    far = send(block_out.at[1], block_in.at[1], across(1))
    block_ref[0] = block[0:rows]
    block_ref[1] = block[2 * rows:3 * rows]
    turnw_ref[:, rows:4 * rows] = jnp.transpose(weighted).astype(BF16)
    loss = loss + total(softplus)
    grad_bias = grad_bias + total(dlogit)
    grad_scale = grad_scale + total(weighted * similar)
    far.wait_recv()
    block_out[2] = (block_ref[1] + block_in[1].astype(F32)).astype(BF16)
    wide = send(block_out.at[2], block_in.at[2], across(2))

    odd = matmul(turnw_ref[0:4 * rows], img_set[...]).astype(BF16)
    gtx_out[...] = odd.reshape(gtx_out.shape)
    gtx_arrive = [
        send(gtx_out.at[k], gtx_in.at[k], along(1)) for k in (1, 2, 3, 0)
    ]
    gtx_ref[...] = matmul(turnw_ref[4 * rows:8 * rows], img_set[...]).reshape(gtx_ref.shape)

    near.wait_recv()
    wide.wait_recv()
    img_proj = proj_ref[...]
    grad = block_ref[0] + block_in[0].astype(F32) + block_in[2].astype(F32)
    product = jnp.sum(img_proj * grad, axis=1, keepdims=True)
    grad = grad / img_len - img_proj * product / (img_len * img_len * img_len)
    grad_set[0] = grad.astype(BF16)
    grad_arrive = {}
    for r in (4, 6, 2, 1):
        grad_arrive[r] = send(grad_set.at[0], grad_set.at[r], along(r))

    gtz_arrive = {}
    third = full_ref.shape[0] // 3
    for k in (1, 2, 3):
        gtx_arrive[k - 1].wait_recv()
        gtz_out[k] = (gtx_ref[k] + gtx_in[k].astype(F32)).astype(BF16)
        gtz_arrive[k] = send(gtz_out.at[k], gtz_in.at[k], along(2 * k))
        grad_arrive[2 * k].wait_recv()
        grad_arrive[2 * k + 1] = send(grad_set.at[2 * k], grad_set.at[2 * k + 1], along(1))
        part = slice((k - 1) * third, k * third)
        back_ref[:, part] = matmul_nt(grad_set[0], full_ref[part, :])

    grad_norm = back_ref[...]
    img_hat = hat_ref[...]
    img_gain_sum = jnp.sum(grad_norm * img_hat, axis=0, keepdims=True)
    scaled = grad_norm * igain_ref[...]
    gif_ref[...] = img_inv * (
        scaled
        - jnp.mean(scaled, axis=1, keepdims=True)
        - img_hat * jnp.mean(scaled * img_hat, axis=1, keepdims=True)
    )

    grad_proj = matmul(turned_in[0], grad_set[0])
    for r in (2, 4, 6):
        turned_arrive[r].wait_recv()
        grad_proj = grad_proj + matmul(turned_in[r], grad_set[r])
    gproj_ref[...] = grad_proj

    gtx_arrive[3].wait_recv()
    grad = gtx_ref[0] + gtx_in[0].astype(F32)
    for k in (1, 2, 3):
        gtz_arrive[k].wait_recv()
        grad = grad + gtz_in[k].astype(F32)
    product = jnp.sum(txt_scaled * grad, axis=1, keepdims=True)
    grad = grad / txt_len - txt_scaled * product / (txt_len * txt_len * txt_len)
    txt_gain_sum = jnp.sum(grad * txt_hat, axis=0, keepdims=True)
    img_tiles = img_ref.shape[1] // 128
    txt_tiles = txt_ref.shape[1] // 128
    small_ref[...] = jnp.zeros_like(small_ref)
    for k in range(img_tiles):
        small_ref[k:k + 1, :] = img_gain_sum[:, k * 128:(k + 1) * 128]
    for k in range(txt_tiles):
        at = img_tiles + k
        small_ref[at:at + 1, :] = txt_gain_sum[:, k * 128:(k + 1) * 128]
    at = img_tiles + txt_tiles
    lanes = lax.broadcasted_iota(jnp.int32, (1, 128), 1)
    small_ref[at:at + 1, :] = jnp.where(
        lanes == 0, loss, jnp.where(lanes == 1, grad_scale, jnp.where(lanes == 2, grad_bias, 0.0))
    )
    small_arrive = [send(small_ref, small_in.at[b], across(r)) for r in (1, 2, 3)]

    scaled = grad * tgain_ref[...]
    gtf_ref[...] = txt_inv * (
        scaled
        - jnp.mean(scaled, axis=1, keepdims=True)
        - txt_hat * jnp.mean(scaled * txt_hat, axis=1, keepdims=True)
    )

    for r in (1, 3, 5, 7):
        turned_arrive[r].wait_recv()
        grad_arrive[r].wait_recv()
    mine = pl.ds(pl.multiple_of(core * half, 16), half)
    other = pl.ds(pl.multiple_of((1 - core) * half, 16), half)
    span_width = gproj_ref.shape[1] // 3
    spans = [slice(k * span_width, (k + 1) * span_width) for k in range(3)]
    gp_first = []
    for k, span in enumerate(spans):
        grad_proj = gproj_ref[:, span]
        for r in (1, 3, 5, 7):
            grad_proj = grad_proj + matmul(turned_in[r], grad_set[r, :, span])
        gproj_ref[:, span] = grad_proj
        gp_first.append(send(gproj_ref.at[other, span], gp_in.at[k], across(1)))

    small_in[b] = small_ref[...]
    for copy in small_arrive:
        copy.wait_recv()
    mid_ref[...] = (small_in[0] + small_in[1]) + (small_in[2] + small_in[3])
    mid_arrive = [send(mid_ref, mid_in.at[f], along(r)) for r in range(1, 8)]
    mid_in[f] = mid_ref[...]

    gp_second = []
    for k, span in enumerate(spans):
        gp_first[k].wait_recv()
        gp_out[k] = (gproj_ref[mine, span] + gp_in[k]).astype(BF16)
        gp_second.append(send(gp_out.at[k], gp_far.at[k], across(2)))
    gp_third = []
    for k, span in enumerate(spans):
        gp_second[k].wait_recv()
        gp_sum[k] = gp_out[k].astype(F32) + gp_far[k].astype(F32)
        gp_third.append(send(gp_sum.at[k], gp_end.at[k], across(1)))
        gproj_ref[mine, span] = gp_sum[k]

    for copy in mid_arrive:
        copy.wait_recv()
    sums = mid_in[0]
    for k in range(1, 8):
        sums = sums + mid_in[k]
    for k in range(img_tiles):
        gig_ref[:, k * 128:(k + 1) * 128] = sums[k:k + 1, :]
    for k in range(txt_tiles):
        at = img_tiles + k
        gtg_ref[:, k * 128:(k + 1) * 128] = sums[at:at + 1, :]
    at = img_tiles + txt_tiles
    loss_ref[...] = sums[at:at + 1, 0:1] / batch_total
    gscale_ref[...] = sums[at:at + 1, 1:2]
    gbias_ref[...] = sums[at:at + 1, 2:3]

    for k, span in enumerate(spans):
        gp_third[k].wait_recv()
        gp_first[k].wait_send()
        gproj_ref[other, span] = gp_end[k]

    for copy in copies:
        if not any(copy is first for first in gp_first):
            copy.wait_send()


def fused_shards(img_feat, txt_feat, partner, projection, img_gain, txt_gain, log_scale, logit_bias):
    rows, width = img_feat.shape
    emb = txt_feat.shape[1]
    depth = projection.shape[0]
    batch_total = rows * lax.axis_size("blk") * lax.axis_size("fsdp")
    small_rows = -(-((width + emb) // 128 + 1) // 8) * 8
    scalar = jax.ShapeDtypeStruct((1, 1), F32)
    vmem = pltpu.VMEM
    outs = pl.pallas_call(
        functools.partial(kernel, batch_total),
        out_shape=(
            scalar,
            scalar,
            scalar,
            jax.ShapeDtypeStruct((depth, emb), F32),
            jax.ShapeDtypeStruct((1, width), F32),
            jax.ShapeDtypeStruct((1, emb), F32),
            jax.ShapeDtypeStruct((rows, width), F32),
            jax.ShapeDtypeStruct((rows, emb), F32),
        ),
        in_specs=[
            pl.BlockSpec(memory_space=vmem if k in (2, 6, 7) else pl.ANY) for k in range(8)
        ],
        out_specs=tuple([pl.BlockSpec(memory_space=vmem)] * 8),
        scratch_shapes=[
            vmem((rows, width), BF16),
            vmem((rows, emb), BF16),
            vmem((1, width), F32),
            vmem((1, emb), F32),
            vmem((width, emb), BF16),
            vmem((rows, width), BF16),
            vmem((rows, width), F32),
            vmem((width, rows), BF16),
            vmem((8, depth, rows), BF16),
            vmem((rows, emb), F32),
            vmem((8, rows, emb), BF16),
            vmem((4 * rows, emb), BF16),
            vmem((4 * rows, 8 * rows), BF16),
            vmem((8 * rows, 4 * rows), BF16),
            vmem((2, rows, emb), F32),
            vmem((3, rows, emb), BF16),
            vmem((3, rows, emb), BF16),
            vmem((4, rows, emb), F32),
            vmem((4, rows, emb), BF16),
            vmem((4, rows, emb), BF16),
            vmem((4, rows, emb), BF16),
            vmem((4, rows, emb), BF16),
            vmem((8, rows, emb), BF16),
            vmem((3, depth // 2, emb // 3), F32),
            vmem((3, depth // 2, emb // 3), BF16),
            vmem((3, depth // 2, emb // 3), BF16),
            vmem((3, depth // 2, emb // 3), F32),
            vmem((3, depth // 2, emb // 3), F32),
            vmem((small_rows, 128), F32),
            vmem((4, small_rows, 128), F32),
            vmem((small_rows, 128), F32),
            vmem((8, small_rows, 128), F32),
            vmem((rows, width), F32),
            pltpu.SemaphoreType.DMA((5,)),
            pltpu.SemaphoreType.DMA((90,)),
            pltpu.SemaphoreType.DMA((90,)),
        ],
        compiler_params=pltpu.CompilerParams(
            collective_id=0, has_side_effects=True, vmem_limit_bytes=58 * 1024 * 1024
        ),
    )(
        img_feat,
        txt_feat,
        partner.reshape(rows, 1),
        projection,
        img_gain.reshape(1, width),
        txt_gain.reshape(1, emb),
        log_scale.reshape(1, 1),
        logit_bias.reshape(1, 1),
    )
    loss, grad_scale, grad_bias, grad_proj, img_sum, txt_sum, img_grad, txt_grad = outs
    return (
        loss.reshape(1),
        grad_scale.reshape(1),
        grad_bias.reshape(1),
        grad_proj,
        img_sum.reshape(width),
        txt_sum.reshape(emb),
        img_grad,
        txt_grad,
    )


def solution(mesh):
    placed = (
        P(("blk", "fsdp"), None),
        P(("blk", "fsdp"), None),
        P(("blk", "fsdp")),
        P("fsdp", None),
        P(),
        P(),
        P(),
        P(),
    )
    fused = mesh.shape["blk"] == 4 and mesh.shape["fsdp"] == 8
    return jax.shard_map(
        fused_shards if fused else shards,
        mesh=mesh,
        in_specs=placed,
        out_specs=(
            P(),
            P(),
            P(),
            P("fsdp", None),
            P(),
            P(),
            P(("blk", "fsdp"), None),
            P(("blk", "fsdp"), None),
        ),
        check_vma=False,
    )
```

```python
import functools

import jax
import jax.numpy as jnp
from jax import lax
from jax.experimental import pallas as pl
from jax.experimental.pallas import tpu as pltpu
from jax.sharding import PartitionSpec as P

EPSILON = 1e-06


def layer_norm(features):
    values = features.astype(jnp.float32)
    centered = values - jnp.mean(values, axis=1, keepdims=True)
    inverse = lax.rsqrt(jnp.mean(centered * centered, axis=1, keepdims=True) + EPSILON)
    return (centered * inverse, inverse)


def layer_norm_back(upstream, normed, inverse, gains):
    scaled = upstream * gains
    return inverse * (
        scaled
        - jnp.mean(scaled, axis=1, keepdims=True)
        - normed * jnp.mean(scaled * normed, axis=1, keepdims=True)
    )


def unit_rows(values):
    length = jnp.sqrt(jnp.sum(values * values, axis=1, keepdims=True) + EPSILON)
    return (values / length, length)


def unit_rows_back(upstream, values, length):
    product = jnp.sum(values * upstream, axis=1, keepdims=True)
    return upstream / length - values * product / (length * length * length)


def pair_terms(img_set, txt_set, targets, temper, offset, batch_total):
    similar = lax.dot_general(
        img_set, txt_set, (((1,), (1,)), ((), ())), preferred_element_type=jnp.float32
    )
    columns = lax.broadcasted_iota(jnp.int32, similar.shape, 1)
    labels = jnp.where(columns == targets[:, None], 1.0, -1.0).astype(jnp.float32)
    margin = labels * (temper * similar + offset)
    dlogit = -labels * jax.nn.sigmoid(-margin) / batch_total
    weighted = (temper * dlogit).astype(jnp.bfloat16)
    partial_sums = (
        jnp.sum(jax.nn.softplus(-margin)),
        jnp.sum(dlogit),
        jnp.sum(dlogit * temper * similar),
    )
    return (weighted, partial_sums)


def shards(img_feat, txt_feat, partner, projection, img_gain, txt_gain, log_scale, logit_bias):
    local_rows = img_feat.shape[0]
    group_count = lax.axis_size("blk")
    member_count = lax.axis_size("fsdp")
    batch_total = local_rows * group_count * member_count
    group_index = lax.axis_index("blk")
    member_index = lax.axis_index("fsdp")
    temper = jnp.exp(log_scale[0])
    offset = logit_bias[0]
    img_hat, img_inv = layer_norm(img_feat)
    img_norm = (img_hat * img_gain).astype(jnp.bfloat16)
    full_proj = lax.all_gather(projection, "fsdp", axis=0, tiled=True)
    img_proj = jnp.dot(img_norm, full_proj, preferred_element_type=jnp.float32)
    img_unit, img_len = unit_rows(img_proj)
    img_emb = img_unit.astype(jnp.bfloat16)
    txt_hat, txt_inv = layer_norm(txt_feat)
    txt_scaled = txt_hat * txt_gain
    txt_unit, txt_len = unit_rows(txt_scaled)
    txt_emb = txt_unit.astype(jnp.bfloat16)
    own_offsets = partner - (group_index * member_count + member_index) * local_rows
    txt_set = lax.all_gather(txt_emb, "fsdp", axis=0, tiled=True)
    block_targets = own_offsets + member_index * local_rows
    block_rows = img_emb.shape[0]
    set_rows = group_count * block_rows
    img_set = lax.all_gather(img_emb, "blk", axis=0, tiled=True)
    targets = jnp.full((set_rows,), -1, jnp.int32)
    targets = lax.dynamic_update_slice(targets, block_targets, (group_index * block_rows,))
    weighted, partial_sums = pair_terms(img_set, txt_set, targets, temper, offset, batch_total)
    grad_block = lax.psum_scatter(
        jnp.dot(weighted, txt_set, preferred_element_type=jnp.float32),
        "blk",
        scatter_dimension=0,
        tiled=True,
    )
    grad_txt_emb = lax.psum_scatter(
        lax.dot_general(
            weighted, img_set, (((0,), (0,)), ((), ())), preferred_element_type=jnp.float32
        ),
        "fsdp",
        scatter_dimension=0,
        tiled=True,
    )
    grad_img_proj = unit_rows_back(grad_block, img_proj, img_len).astype(jnp.bfloat16)
    grad_proj = lax.psum_scatter(
        lax.dot_general(
            img_norm, grad_img_proj, (((0,), (0,)), ((), ())), preferred_element_type=jnp.float32
        ),
        "fsdp",
        scatter_dimension=0,
        tiled=True,
    )
    grad_proj = lax.psum(grad_proj, "blk")
    grad_img_norm = lax.dot_general(
        grad_img_proj, full_proj, (((1,), (1,)), ((), ())), preferred_element_type=jnp.float32
    )
    grad_img_feat = layer_norm_back(grad_img_norm, img_hat, img_inv, img_gain)
    grad_txt_scaled = unit_rows_back(grad_txt_emb, txt_scaled, txt_len)
    grad_txt_feat = layer_norm_back(grad_txt_scaled, txt_hat, txt_inv, txt_gain)
    totals = lax.psum(
        (
            partial_sums[0],
            partial_sums[1],
            partial_sums[2],
            jnp.sum(grad_img_norm * img_hat, axis=0),
            jnp.sum(grad_txt_scaled * txt_hat, axis=0),
        ),
        ("blk", "fsdp"),
    )
    return (
        (totals[0] / batch_total).reshape(1),
        totals[2].reshape(1),
        totals[1].reshape(1),
        grad_proj,
        totals[3],
        totals[4],
        grad_img_feat,
        grad_txt_feat,
    )


MESH = pl.DeviceIdType.MESH
BF16 = jnp.bfloat16
F32 = jnp.float32


def txt_slot(distance):
    return distance // 2 if distance % 2 else 4 + distance // 2


def flip(bit, yes):
    return 1 - bit if yes else bit


def matmul(left, right):
    return jnp.dot(left, right, preferred_element_type=F32)


def matmul_nt(left, right):
    return lax.dot_general(left, right, (((1,), (1,)), ((), ())), preferred_element_type=F32)


def pair_math(similar, labels, temper, offset, batch_total):
    margin = labels * (temper * similar + offset)
    small = jnp.exp(-jnp.abs(margin))
    chance = jnp.where(margin >= 0.0, small, 1.0) / (1.0 + small)
    dlogit = -labels * chance / batch_total
    softplus = jnp.maximum(-margin, 0.0) + jnp.log1p(small)
    return dlogit, softplus


def total(values):
    return jnp.sum(jnp.sum(values, axis=0, keepdims=True), axis=1, keepdims=True)


def kernel(
    batch_total, img_hbm, txt_hbm, goal_ref, part_ref, igain_flat, tgain_flat, scale_ref, bias_ref,
    loss_ref, gscale_ref, gbias_ref, gproj_ref, gig_ref, gtg_ref, gif_ref, gtf_ref,
    img_ref, txt_ref, igain_ref, tgain_ref, full_ref, norm_ref, hat_ref, turned_ref, turned_in, proj_ref,
    txt_set, img_set, weight_ref, turnw_ref, block_ref, block_out, block_in,
    gtx_ref, gtx_out, gtx_in, gtz_out, gtz_in, grad_set,
    gp_in, gp_out, gp_far, gp_sum, gp_end, small_ref, small_in, mid_ref, mid_in, back_ref,
    load_sem, send_sem, recv_sem,
):
    rows = img_ref.shape[0]
    depth = part_ref.shape[0]
    quarter = depth // 4
    half = depth // 2
    b = lax.axis_index("blk")
    f = lax.axis_index("fsdp")
    core, y = b % 2, b // 2
    x, z_low, z_high = f % 2, (f // 2) % 2, f // 4

    def member(r):
        return (flip(z_high, r & 4) * 2 + flip(z_low, r & 2)) * 2 + flip(x, r & 1)

    def group(r):
        return flip(y, r & 2) * 2 + flip(core, r & 1)

    own_rows = full_ref.at[pl.ds(pl.multiple_of(f * depth, 16), depth), :]
    loads = []
    for source, target in (
        (txt_hbm, txt_ref), (img_hbm, img_ref), (part_ref, own_rows),
    ):
        loads.append(pltpu.make_async_copy(source, target, load_sem.at[len(loads)]))
        loads[-1].start()

    barrier = pltpu.get_barrier_semaphore()
    for r in range(1, 8):
        pl.semaphore_signal(barrier, inc=1, device_id=(b, member(r)), device_id_type=MESH)
    for r in range(1, 4):
        pl.semaphore_signal(barrier, inc=1, device_id=(group(r), f), device_id_type=MESH)
    pl.semaphore_wait(barrier, 10)

    copies = []

    def send(source, target, to):
        k = len(copies)
        copy = pltpu.make_async_remote_copy(
            src_ref=source, dst_ref=target, send_sem=send_sem.at[k], recv_sem=recv_sem.at[k],
            device_id=to, device_id_type=MESH,
        )
        copy.start()
        copies.append(copy)
        return copy

    def along(r):
        return (b, member(r))

    def across(r):
        return (group(r), f)

    def piece(r, q):
        start = member(r) * depth + group(q) * quarter
        return full_ref.at[pl.ds(pl.multiple_of(start, 16), quarter), :]

    own_piece = part_ref.at[pl.ds(pl.multiple_of(b * quarter, 16), quarter), :]
    arrive = {}
    for r in (4, 6, 2, 1):
        arrive[r, 0] = send(own_piece, piece(0, 0), along(r))

    loads[0].wait()
    tgain_ref[...] = tgain_flat[...].reshape(tgain_ref.shape)
    igain_ref[...] = igain_flat[...].reshape(igain_ref.shape)
    values = txt_ref[...].astype(F32)
    centered = values - jnp.mean(values, axis=1, keepdims=True)
    txt_inv = lax.rsqrt(jnp.mean(centered * centered, axis=1, keepdims=True) + EPSILON)
    txt_hat = centered * txt_inv
    txt_scaled = txt_hat * tgain_ref[...]
    txt_len = jnp.sqrt(jnp.sum(txt_scaled * txt_scaled, axis=1, keepdims=True) + EPSILON)
    txt_set[txt_slot(0)] = (txt_scaled / txt_len).astype(BF16)
    txt_arrive = {}
    for r in (4, 6, 2, 1):
        txt_arrive[r] = send(txt_set.at[txt_slot(0)], txt_set.at[txt_slot(r)], along(r))

    def spread(r):
        arrive[r, 0].wait_recv()
        if r % 2 == 0:
            arrive[r + 1, 0] = send(piece(r, 0), piece(r, 0), along(1))
        arrive[r, 2] = send(piece(r, 0), piece(r, 0), across(2))
        arrive[r, 1] = send(piece(r, 0), piece(r, 0), across(1))

    spread(2)

    loads[1].wait()
    values = img_ref[...].astype(F32)
    centered = values - jnp.mean(values, axis=1, keepdims=True)
    img_inv = lax.rsqrt(jnp.mean(centered * centered, axis=1, keepdims=True) + EPSILON)
    img_hat = centered * img_inv
    hat_ref[...] = img_hat
    img_norm = img_hat * igain_ref[...]
    norm_ref[...] = img_norm.astype(BF16)
    for r in (4, 6):
        spread(r)
    turned_ref[...] = jnp.transpose(hat_ref[...] * igain_ref[...]).astype(BF16)
    for r in (1, 3, 5, 7):
        spread(r)
    for r in (2, 4, 6):
        txt_arrive[r].wait_recv()
        txt_arrive[r + 1] = send(
            txt_set.at[txt_slot(r)], txt_set.at[txt_slot(r + 1)], along(1)
        )
    for r in (2, 4, 6, 1, 3, 5, 7):
        arrive[r, 2].wait_recv()
        arrive[r, 3] = send(piece(r, 2), piece(r, 2), across(1))
    loads[2].wait()
    img_proj = None
    for r in (0, 2, 4, 6):
        for s in (r, r + 1):
            if s:
                arrive[s, 1].wait_recv()
                arrive[s, 3].wait_recv()
        pair = member(r) // 2 * (2 * depth)
        pair = pl.ds(pl.multiple_of(pair, 128), 2 * depth)
        term = matmul(norm_ref[:, pair], full_ref[pair, :])
        img_proj = term if img_proj is None else img_proj + term
    proj_ref[...] = img_proj
    img_len = jnp.sqrt(jnp.sum(img_proj * img_proj, axis=1, keepdims=True) + EPSILON)
    img_set[0:rows] = (img_proj / img_len).astype(BF16)
    own = img_set.at[0:rows]
    from_y = send(own, img_set.at[2 * rows:3 * rows], across(2))
    from_core = send(own, img_set.at[rows:2 * rows], across(1))
    turned_arrive = {}
    for r in (2, 4, 6, 1, 3, 5, 7):
        rows_of = pl.ds(pl.multiple_of(member(r) * depth, 16), depth)
        turned_arrive[r] = send(turned_ref.at[rows_of, :], turned_in.at[r], along(r))
    turned_in[0] = turned_ref[pl.ds(pl.multiple_of(f * depth, 16), depth), :]

    for r in (1, 3, 5, 7):
        txt_arrive[r].wait_recv()
    txt_all = txt_set[...].reshape(8 * rows, txt_set.shape[2])
    temper = jnp.exp(scale_ref[...])
    offset = bias_ref[...]
    similar = matmul_nt(img_set[0:rows], txt_all)
    columns = lax.broadcasted_iota(jnp.int32, similar.shape, 1)
    goal = goal_ref[...] - (b * 8 + f) * rows + txt_slot(0) * rows
    labels = jnp.where(columns == goal, 1.0, -1.0).astype(F32)
    dlogit, softplus = pair_math(similar, labels, temper, offset, batch_total)
    weighted = temper * dlogit
    weight_ref[0:rows] = weighted.astype(BF16)
    turnw_ref[:, 0:rows] = jnp.transpose(weighted).astype(BF16)
    loss = total(softplus)
    grad_bias = total(dlogit)
    grad_scale = total(weighted * similar)
    from_y.wait_recv()
    from_far = send(img_set.at[2 * rows:3 * rows], img_set.at[3 * rows:4 * rows], across(1))
    from_core.wait_recv()
    from_far.wait_recv()
    similar = matmul_nt(img_set[rows:4 * rows], txt_all)
    dlogit, softplus = pair_math(similar, -1.0, temper, offset, batch_total)
    weighted = temper * dlogit
    weight_ref[rows:4 * rows] = weighted.astype(BF16)
    block = matmul(weight_ref[...], txt_all)
    block_out[0] = block[rows:2 * rows].astype(BF16)
    block_out[1] = block[3 * rows:4 * rows].astype(BF16)
    near = send(block_out.at[0], block_in.at[0], across(1))
    far = send(block_out.at[1], block_in.at[1], across(1))
    block_ref[0] = block[0:rows]
    block_ref[1] = block[2 * rows:3 * rows]
    turnw_ref[:, rows:4 * rows] = jnp.transpose(weighted).astype(BF16)
    loss = loss + total(softplus)
    grad_bias = grad_bias + total(dlogit)
    grad_scale = grad_scale + total(weighted * similar)
    far.wait_recv()
    block_out[2] = (block_ref[1] + block_in[1].astype(F32)).astype(BF16)
    wide = send(block_out.at[2], block_in.at[2], across(2))

    odd = matmul(turnw_ref[0:4 * rows], img_set[...]).astype(BF16)
    gtx_out[...] = odd.reshape(gtx_out.shape)
    gtx_arrive = [
        send(gtx_out.at[k], gtx_in.at[k], along(1)) for k in (1, 2, 3, 0)
    ]
    gtx_ref[...] = matmul(turnw_ref[4 * rows:8 * rows], img_set[...]).reshape(gtx_ref.shape)

    near.wait_recv()
    wide.wait_recv()
    img_proj = proj_ref[...]
    grad = block_ref[0] + block_in[0].astype(F32) + block_in[2].astype(F32)
    product = jnp.sum(img_proj * grad, axis=1, keepdims=True)
    grad = grad / img_len - img_proj * product / (img_len * img_len * img_len)
    grad_set[0] = grad.astype(BF16)
    grad_arrive = {}
    for r in (4, 6, 2, 1):
        grad_arrive[r] = send(grad_set.at[0], grad_set.at[r], along(r))

    gtz_arrive = {}
    third = full_ref.shape[0] // 3
    for k in (1, 2, 3):
        gtx_arrive[k - 1].wait_recv()
        gtz_out[k] = (gtx_ref[k] + gtx_in[k].astype(F32)).astype(BF16)
        gtz_arrive[k] = send(gtz_out.at[k], gtz_in.at[k], along(2 * k))
        grad_arrive[2 * k].wait_recv()
        grad_arrive[2 * k + 1] = send(grad_set.at[2 * k], grad_set.at[2 * k + 1], along(1))
        part = slice((k - 1) * third, k * third)
        back_ref[:, part] = matmul_nt(grad_set[0], full_ref[part, :])

    grad_norm = back_ref[...]
    img_hat = hat_ref[...]
    img_gain_sum = jnp.sum(grad_norm * img_hat, axis=0, keepdims=True)
    scaled = grad_norm * igain_ref[...]
    gif_ref[...] = img_inv * (
        scaled
        - jnp.mean(scaled, axis=1, keepdims=True)
        - img_hat * jnp.mean(scaled * img_hat, axis=1, keepdims=True)
    )

    grad_proj = matmul(turned_in[0], grad_set[0])
    for r in (2, 4, 6):
        turned_arrive[r].wait_recv()
        grad_proj = grad_proj + matmul(turned_in[r], grad_set[r])
    gproj_ref[...] = grad_proj

    gtx_arrive[3].wait_recv()
    grad = gtx_ref[0] + gtx_in[0].astype(F32)
    for k in (1, 2, 3):
        gtz_arrive[k].wait_recv()
        grad = grad + gtz_in[k].astype(F32)
    product = jnp.sum(txt_scaled * grad, axis=1, keepdims=True)
    grad = grad / txt_len - txt_scaled * product / (txt_len * txt_len * txt_len)
    txt_gain_sum = jnp.sum(grad * txt_hat, axis=0, keepdims=True)
    img_tiles = img_ref.shape[1] // 128
    txt_tiles = txt_ref.shape[1] // 128
    small_ref[...] = jnp.zeros_like(small_ref)
    for k in range(img_tiles):
        small_ref[k:k + 1, :] = img_gain_sum[:, k * 128:(k + 1) * 128]
    for k in range(txt_tiles):
        at = img_tiles + k
        small_ref[at:at + 1, :] = txt_gain_sum[:, k * 128:(k + 1) * 128]
    at = img_tiles + txt_tiles
    lanes = lax.broadcasted_iota(jnp.int32, (1, 128), 1)
    small_ref[at:at + 1, :] = jnp.where(
        lanes == 0, loss, jnp.where(lanes == 1, grad_scale, jnp.where(lanes == 2, grad_bias, 0.0))
    )
    small_arrive = [send(small_ref, small_in.at[b], across(r)) for r in (1, 2, 3)]

    scaled = grad * tgain_ref[...]
    gtf_ref[...] = txt_inv * (
        scaled
        - jnp.mean(scaled, axis=1, keepdims=True)
        - txt_hat * jnp.mean(scaled * txt_hat, axis=1, keepdims=True)
    )

    for r in (1, 3, 5, 7):
        turned_arrive[r].wait_recv()
        grad_arrive[r].wait_recv()
    mine = pl.ds(pl.multiple_of(core * half, 16), half)
    other = pl.ds(pl.multiple_of((1 - core) * half, 16), half)
    span_width = gproj_ref.shape[1] // 3
    spans = [slice(k * span_width, (k + 1) * span_width) for k in range(3)]
    gp_first = []
    for k, span in enumerate(spans):
        grad_proj = gproj_ref[:, span]
        for r in (1, 3, 5, 7):
            grad_proj = grad_proj + matmul(turned_in[r], grad_set[r, :, span])
        gproj_ref[:, span] = grad_proj
        gp_first.append(send(gproj_ref.at[other, span], gp_in.at[k], across(1)))

    small_in[b] = small_ref[...]
    for copy in small_arrive:
        copy.wait_recv()
    mid_ref[...] = (small_in[0] + small_in[1]) + (small_in[2] + small_in[3])
    mid_arrive = [send(mid_ref, mid_in.at[f], along(r)) for r in range(1, 8)]
    mid_in[f] = mid_ref[...]

    gp_second = []
    for k, span in enumerate(spans):
        gp_first[k].wait_recv()
        gp_out[k] = (gproj_ref[mine, span] + gp_in[k]).astype(BF16)
        gp_second.append(send(gp_out.at[k], gp_far.at[k], across(2)))
    gp_third = []
    for k, span in enumerate(spans):
        gp_second[k].wait_recv()
        gp_sum[k] = gp_out[k].astype(F32) + gp_far[k].astype(F32)
        gp_third.append(send(gp_sum.at[k], gp_end.at[k], across(1)))
        gproj_ref[mine, span] = gp_sum[k]

    for copy in mid_arrive:
        copy.wait_recv()
    sums = mid_in[0]
    for k in range(1, 8):
        sums = sums + mid_in[k]
    for k in range(img_tiles):
        gig_ref[k * 128:(k + 1) * 128] = sums[k]
    for k in range(txt_tiles):
        at = img_tiles + k
        gtg_ref[k * 128:(k + 1) * 128] = sums[at]
    at = img_tiles + txt_tiles
    loss_ref[...] = sums[at:at + 1, 0:1] / batch_total
    gscale_ref[...] = sums[at:at + 1, 1:2]
    gbias_ref[...] = sums[at:at + 1, 2:3]

    for k, span in enumerate(spans):
        gp_third[k].wait_recv()
        gp_first[k].wait_send()
        gproj_ref[other, span] = gp_end[k]

    for copy in copies:
        if not any(copy is first for first in gp_first):
            copy.wait_send()


def fused_shards(img_feat, txt_feat, partner, projection, img_gain, txt_gain, log_scale, logit_bias):
    rows, width = img_feat.shape
    emb = txt_feat.shape[1]
    depth = projection.shape[0]
    batch_total = rows * lax.axis_size("blk") * lax.axis_size("fsdp")
    small_rows = -(-((width + emb) // 128 + 1) // 8) * 8
    scalar = jax.ShapeDtypeStruct((1, 1), F32)
    vmem = pltpu.VMEM
    outs = pl.pallas_call(
        functools.partial(kernel, batch_total),
        out_shape=(
            scalar,
            scalar,
            scalar,
            jax.ShapeDtypeStruct((depth, emb), F32),
            jax.ShapeDtypeStruct((width,), F32),
            jax.ShapeDtypeStruct((emb,), F32),
            jax.ShapeDtypeStruct((rows, width), F32),
            jax.ShapeDtypeStruct((rows, emb), F32),
        ),
        in_specs=[
            pl.BlockSpec(memory_space=pltpu.HBM if k in (0, 1, 3) else vmem) for k in range(8)
        ],
        out_specs=tuple([pl.BlockSpec(memory_space=vmem)] * 8),
        scratch_shapes=[
            vmem((rows, width), BF16),
            vmem((rows, emb), BF16),
            vmem((1, width), F32),
            vmem((1, emb), F32),
            vmem((width, emb), BF16),
            vmem((rows, width), BF16),
            vmem((rows, width), F32),
            vmem((width, rows), BF16),
            vmem((8, depth, rows), BF16),
            vmem((rows, emb), F32),
            vmem((8, rows, emb), BF16),
            vmem((4 * rows, emb), BF16),
            vmem((4 * rows, 8 * rows), BF16),
            vmem((8 * rows, 4 * rows), BF16),
            vmem((2, rows, emb), F32),
            vmem((3, rows, emb), BF16),
            vmem((3, rows, emb), BF16),
            vmem((4, rows, emb), F32),
            vmem((4, rows, emb), BF16),
            vmem((4, rows, emb), BF16),
            vmem((4, rows, emb), BF16),
            vmem((4, rows, emb), BF16),
            vmem((8, rows, emb), BF16),
            vmem((3, depth // 2, emb // 3), F32),
            vmem((3, depth // 2, emb // 3), BF16),
            vmem((3, depth // 2, emb // 3), BF16),
            vmem((3, depth // 2, emb // 3), F32),
            vmem((3, depth // 2, emb // 3), F32),
            vmem((small_rows, 128), F32),
            vmem((4, small_rows, 128), F32),
            vmem((small_rows, 128), F32),
            vmem((8, small_rows, 128), F32),
            vmem((rows, width), F32),
            pltpu.SemaphoreType.DMA((5,)),
            pltpu.SemaphoreType.DMA((90,)),
            pltpu.SemaphoreType.DMA((90,)),
        ],
        compiler_params=pltpu.CompilerParams(
            collective_id=0, has_side_effects=True, vmem_limit_bytes=48 * 1024 * 1024
        ),
    )(
        img_feat,
        txt_feat,
        partner.reshape(rows, 1),
        projection,
        img_gain,
        txt_gain,
        log_scale.reshape(1, 1),
        logit_bias.reshape(1, 1),
    )
    loss, grad_scale, grad_bias, grad_proj, img_sum, txt_sum, img_grad, txt_grad = outs
    return (
        loss.reshape(1),
        grad_scale.reshape(1),
        grad_bias.reshape(1),
        grad_proj,
        img_sum,
        txt_sum,
        img_grad,
        txt_grad,
    )


def solution(mesh):
    placed = (
        P(("blk", "fsdp"), None),
        P(("blk", "fsdp"), None),
        P(("blk", "fsdp")),
        P("fsdp", None),
        P(),
        P(),
        P(),
        P(),
    )
    fused = mesh.shape["blk"] == 4 and mesh.shape["fsdp"] == 8
    return jax.shard_map(
        fused_shards if fused else shards,
        mesh=mesh,
        in_specs=placed,
        out_specs=(
            P(),
            P(),
            P(),
            P("fsdp", None),
            P(),
            P(),
            P(("blk", "fsdp"), None),
            P(("blk", "fsdp"), None),
        ),
        check_vma=False,
    )
```

```python
import functools

import jax
import jax.numpy as jnp
from jax import lax
from jax.experimental import pallas as pl
from jax.experimental.pallas import tpu as pltpu
from jax.sharding import PartitionSpec as P

EPSILON = 1e-06


def layer_norm(features):
    values = features.astype(jnp.float32)
    centered = values - jnp.mean(values, axis=1, keepdims=True)
    inverse = lax.rsqrt(jnp.mean(centered * centered, axis=1, keepdims=True) + EPSILON)
    return (centered * inverse, inverse)


def layer_norm_back(upstream, normed, inverse, gains):
    scaled = upstream * gains
    return inverse * (
        scaled
        - jnp.mean(scaled, axis=1, keepdims=True)
        - normed * jnp.mean(scaled * normed, axis=1, keepdims=True)
    )


def unit_rows(values):
    length = jnp.sqrt(jnp.sum(values * values, axis=1, keepdims=True) + EPSILON)
    return (values / length, length)


def unit_rows_back(upstream, values, length):
    product = jnp.sum(values * upstream, axis=1, keepdims=True)
    return upstream / length - values * product / (length * length * length)


def pair_terms(img_set, txt_set, targets, temper, offset, batch_total):
    similar = lax.dot_general(
        img_set, txt_set, (((1,), (1,)), ((), ())), preferred_element_type=jnp.float32
    )
    columns = lax.broadcasted_iota(jnp.int32, similar.shape, 1)
    labels = jnp.where(columns == targets[:, None], 1.0, -1.0).astype(jnp.float32)
    margin = labels * (temper * similar + offset)
    dlogit = -labels * jax.nn.sigmoid(-margin) / batch_total
    weighted = (temper * dlogit).astype(jnp.bfloat16)
    partial_sums = (
        jnp.sum(jax.nn.softplus(-margin)),
        jnp.sum(dlogit),
        jnp.sum(dlogit * temper * similar),
    )
    return (weighted, partial_sums)


def shards(img_feat, txt_feat, partner, projection, img_gain, txt_gain, log_scale, logit_bias):
    local_rows = img_feat.shape[0]
    group_count = lax.axis_size("blk")
    member_count = lax.axis_size("fsdp")
    batch_total = local_rows * group_count * member_count
    group_index = lax.axis_index("blk")
    member_index = lax.axis_index("fsdp")
    temper = jnp.exp(log_scale[0])
    offset = logit_bias[0]
    img_hat, img_inv = layer_norm(img_feat)
    img_norm = (img_hat * img_gain).astype(jnp.bfloat16)
    full_proj = lax.all_gather(projection, "fsdp", axis=0, tiled=True)
    img_proj = jnp.dot(img_norm, full_proj, preferred_element_type=jnp.float32)
    img_unit, img_len = unit_rows(img_proj)
    img_emb = img_unit.astype(jnp.bfloat16)
    txt_hat, txt_inv = layer_norm(txt_feat)
    txt_scaled = txt_hat * txt_gain
    txt_unit, txt_len = unit_rows(txt_scaled)
    txt_emb = txt_unit.astype(jnp.bfloat16)
    own_offsets = partner - (group_index * member_count + member_index) * local_rows
    txt_set = lax.all_gather(txt_emb, "fsdp", axis=0, tiled=True)
    block_targets = own_offsets + member_index * local_rows
    block_rows = img_emb.shape[0]
    set_rows = group_count * block_rows
    img_set = lax.all_gather(img_emb, "blk", axis=0, tiled=True)
    targets = jnp.full((set_rows,), -1, jnp.int32)
    targets = lax.dynamic_update_slice(targets, block_targets, (group_index * block_rows,))
    weighted, partial_sums = pair_terms(img_set, txt_set, targets, temper, offset, batch_total)
    grad_block = lax.psum_scatter(
        jnp.dot(weighted, txt_set, preferred_element_type=jnp.float32),
        "blk",
        scatter_dimension=0,
        tiled=True,
    )
    grad_txt_emb = lax.psum_scatter(
        lax.dot_general(
            weighted, img_set, (((0,), (0,)), ((), ())), preferred_element_type=jnp.float32
        ),
        "fsdp",
        scatter_dimension=0,
        tiled=True,
    )
    grad_img_proj = unit_rows_back(grad_block, img_proj, img_len).astype(jnp.bfloat16)
    grad_proj = lax.psum_scatter(
        lax.dot_general(
            img_norm, grad_img_proj, (((0,), (0,)), ((), ())), preferred_element_type=jnp.float32
        ),
        "fsdp",
        scatter_dimension=0,
        tiled=True,
    )
    grad_proj = lax.psum(grad_proj, "blk")
    grad_img_norm = lax.dot_general(
        grad_img_proj, full_proj, (((1,), (1,)), ((), ())), preferred_element_type=jnp.float32
    )
    grad_img_feat = layer_norm_back(grad_img_norm, img_hat, img_inv, img_gain)
    grad_txt_scaled = unit_rows_back(grad_txt_emb, txt_scaled, txt_len)
    grad_txt_feat = layer_norm_back(grad_txt_scaled, txt_hat, txt_inv, txt_gain)
    totals = lax.psum(
        (
            partial_sums[0],
            partial_sums[1],
            partial_sums[2],
            jnp.sum(grad_img_norm * img_hat, axis=0),
            jnp.sum(grad_txt_scaled * txt_hat, axis=0),
        ),
        ("blk", "fsdp"),
    )
    return (
        (totals[0] / batch_total).reshape(1),
        totals[2].reshape(1),
        totals[1].reshape(1),
        grad_proj,
        totals[3],
        totals[4],
        grad_img_feat,
        grad_txt_feat,
    )


MESH = pl.DeviceIdType.MESH
BF16 = jnp.bfloat16
F32 = jnp.float32


def txt_slot(distance):
    return distance // 2 if distance % 2 else 4 + distance // 2


def flip(bit, yes):
    return 1 - bit if yes else bit


def matmul(left, right):
    return jnp.dot(left, right, preferred_element_type=F32)


def matmul_nt(left, right):
    return lax.dot_general(left, right, (((1,), (1,)), ((), ())), preferred_element_type=F32)


def pair_math(similar, labels, temper, offset, batch_total):
    margin = labels * (temper * similar + offset)
    small = jnp.exp(-jnp.abs(margin))
    chance = jnp.where(margin >= 0.0, small, 1.0) / (1.0 + small)
    dlogit = -labels * chance / batch_total
    softplus = jnp.maximum(-margin, 0.0) + jnp.log1p(small)
    return dlogit, softplus


def total(values):
    return jnp.sum(jnp.sum(values, axis=0, keepdims=True), axis=1, keepdims=True)


def kernel(
    batch_total, img_ref, txt_ref, goal_ref, part_ref, igain_flat, tgain_flat, scale_ref, bias_ref,
    loss_ref, gscale_ref, gbias_ref, gproj_ref, gig_ref, gtg_ref, gif_ref, gtf_ref,
    igain_ref, tgain_ref, full_ref, norm_ref, hat_ref, turned_ref, turned_in, proj_ref,
    txt_set, img_set, weight_ref, turnw_ref, block_ref, block_out, block_in,
    gtx_ref, gtx_out, gtx_in, gtz_out, gtz_in, grad_set,
    gp_in, gp_out, gp_far, gp_sum, gp_end, small_ref, small_in, mid_ref, mid_in, send_sem, recv_sem,
):
    rows = img_ref.shape[0]
    depth = part_ref.shape[0]
    quarter = depth // 4
    half = depth // 2
    b = lax.axis_index("blk")
    f = lax.axis_index("fsdp")
    core, y = b % 2, b // 2
    x, z_low, z_high = f % 2, (f // 2) % 2, f // 4

    def member(r):
        return (flip(z_high, r & 4) * 2 + flip(z_low, r & 2)) * 2 + flip(x, r & 1)

    def group(r):
        return flip(y, r & 2) * 2 + flip(core, r & 1)

    barrier = pltpu.get_barrier_semaphore()
    for r in range(1, 8):
        pl.semaphore_signal(barrier, inc=1, device_id=(b, member(r)), device_id_type=MESH)
    for r in range(1, 4):
        pl.semaphore_signal(barrier, inc=1, device_id=(group(r), f), device_id_type=MESH)
    pl.semaphore_wait(barrier, 10)

    copies = []

    def send(source, target, to):
        k = len(copies)
        copy = pltpu.make_async_remote_copy(
            src_ref=source, dst_ref=target, send_sem=send_sem.at[k], recv_sem=recv_sem.at[k],
            device_id=to, device_id_type=MESH,
        )
        copy.start()
        copies.append(copy)
        return copy

    def along(r):
        return (b, member(r))

    def across(r):
        return (group(r), f)

    def piece(r, q):
        start = member(r) * depth + group(q) * quarter
        return full_ref.at[pl.ds(pl.multiple_of(start, 16), quarter), :]

    own_piece = part_ref.at[pl.ds(pl.multiple_of(b * quarter, 16), quarter), :]
    arrive = {}
    for r in (4, 6, 2, 1):
        arrive[r, 0] = send(own_piece, piece(0, 0), along(r))
    full_ref[pl.ds(pl.multiple_of(f * depth, 16), depth), :] = part_ref[...]

    tgain_ref[...] = tgain_flat[...].reshape(tgain_ref.shape)
    igain_ref[...] = igain_flat[...].reshape(igain_ref.shape)

    values = txt_ref[...].astype(F32)
    centered = values - jnp.mean(values, axis=1, keepdims=True)
    txt_inv = lax.rsqrt(jnp.mean(centered * centered, axis=1, keepdims=True) + EPSILON)
    txt_hat = centered * txt_inv
    txt_scaled = txt_hat * tgain_ref[...]
    txt_len = jnp.sqrt(jnp.sum(txt_scaled * txt_scaled, axis=1, keepdims=True) + EPSILON)
    txt_set[txt_slot(0)] = (txt_scaled / txt_len).astype(BF16)
    txt_arrive = {}
    for r in (4, 6, 2, 1):
        txt_arrive[r] = send(txt_set.at[txt_slot(0)], txt_set.at[txt_slot(r)], along(r))

    values = img_ref[...].astype(F32)
    centered = values - jnp.mean(values, axis=1, keepdims=True)
    img_inv = lax.rsqrt(jnp.mean(centered * centered, axis=1, keepdims=True) + EPSILON)
    img_hat = centered * img_inv
    hat_ref[...] = img_hat
    img_norm = img_hat * igain_ref[...]
    norm_ref[...] = img_norm.astype(BF16)
    turned_ref[...] = jnp.transpose(img_norm).astype(BF16)

    for r in (2, 4, 6):
        arrive[r, 0].wait_recv()
        arrive[r + 1, 0] = send(piece(r, 0), piece(r, 0), along(1))
        arrive[r, 2] = send(piece(r, 0), piece(r, 0), across(2))
        arrive[r, 1] = send(piece(r, 0), piece(r, 0), across(1))
    for r in (1, 3, 5, 7):
        arrive[r, 0].wait_recv()
        arrive[r, 2] = send(piece(r, 0), piece(r, 0), across(2))
        arrive[r, 1] = send(piece(r, 0), piece(r, 0), across(1))
    for r in (2, 4, 6):
        txt_arrive[r].wait_recv()
        txt_arrive[r + 1] = send(
            txt_set.at[txt_slot(r)], txt_set.at[txt_slot(r + 1)], along(1)
        )
    for r in (2, 4, 6, 1, 3, 5, 7):
        arrive[r, 2].wait_recv()
        arrive[r, 3] = send(piece(r, 2), piece(r, 2), across(1))
    img_proj = None
    for r in (0, 2, 4, 6):
        for s in (r, r + 1):
            if s:
                arrive[s, 1].wait_recv()
                arrive[s, 3].wait_recv()
        pair = member(r) // 2 * (2 * depth)
        pair = pl.ds(pl.multiple_of(pair, 128), 2 * depth)
        term = matmul(norm_ref[:, pair], full_ref[pair, :])
        img_proj = term if img_proj is None else img_proj + term
    proj_ref[...] = img_proj
    img_len = jnp.sqrt(jnp.sum(img_proj * img_proj, axis=1, keepdims=True) + EPSILON)
    img_set[0:rows] = (img_proj / img_len).astype(BF16)
    own = img_set.at[0:rows]
    from_y = send(own, img_set.at[2 * rows:3 * rows], across(2))
    from_core = send(own, img_set.at[rows:2 * rows], across(1))
    turned_arrive = {}
    for r in (2, 4, 6, 1, 3, 5, 7):
        rows_of = pl.ds(pl.multiple_of(member(r) * depth, 16), depth)
        turned_arrive[r] = send(turned_ref.at[rows_of, :], turned_in.at[r], along(r))
    turned_in[0] = turned_ref[pl.ds(pl.multiple_of(f * depth, 16), depth), :]

    for r in (1, 3, 5, 7):
        txt_arrive[r].wait_recv()
    txt_all = txt_set[...].reshape(8 * rows, txt_set.shape[2])
    temper = jnp.exp(scale_ref[...])
    offset = bias_ref[...]
    similar = matmul_nt(img_set[0:rows], txt_all)
    columns = lax.broadcasted_iota(jnp.int32, similar.shape, 1)
    goal = goal_ref[...] - (b * 8 + f) * rows + txt_slot(0) * rows
    labels = jnp.where(columns == goal, 1.0, -1.0).astype(F32)
    dlogit, softplus = pair_math(similar, labels, temper, offset, batch_total)
    weighted = temper * dlogit
    weight_ref[0:rows] = weighted.astype(BF16)
    turnw_ref[:, 0:rows] = jnp.transpose(weighted).astype(BF16)
    loss = total(softplus)
    grad_bias = total(dlogit)
    grad_scale = total(weighted * similar)
    from_y.wait_recv()
    from_far = send(img_set.at[2 * rows:3 * rows], img_set.at[3 * rows:4 * rows], across(1))
    from_core.wait_recv()
    from_far.wait_recv()
    similar = matmul_nt(img_set[rows:4 * rows], txt_all)
    dlogit, softplus = pair_math(similar, -1.0, temper, offset, batch_total)
    weighted = temper * dlogit
    weight_ref[rows:4 * rows] = weighted.astype(BF16)
    block = matmul(weight_ref[...], txt_all)
    block_out[0] = block[rows:2 * rows].astype(BF16)
    block_out[1] = block[3 * rows:4 * rows].astype(BF16)
    near = send(block_out.at[0], block_in.at[0], across(1))
    far = send(block_out.at[1], block_in.at[1], across(1))
    block_ref[0] = block[0:rows]
    block_ref[1] = block[2 * rows:3 * rows]
    turnw_ref[:, rows:4 * rows] = jnp.transpose(weighted).astype(BF16)
    loss = loss + total(softplus)
    grad_bias = grad_bias + total(dlogit)
    grad_scale = grad_scale + total(weighted * similar)
    far.wait_recv()
    block_out[2] = (block_ref[1] + block_in[1].astype(F32)).astype(BF16)
    wide = send(block_out.at[2], block_in.at[2], across(2))

    odd = matmul(turnw_ref[0:4 * rows], img_set[...]).astype(BF16)
    gtx_out[...] = odd.reshape(gtx_out.shape)
    gtx_arrive = [
        send(gtx_out.at[k], gtx_in.at[k], along(1)) for k in (1, 2, 3, 0)
    ]
    gtx_ref[...] = matmul(turnw_ref[4 * rows:8 * rows], img_set[...]).reshape(gtx_ref.shape)

    near.wait_recv()
    wide.wait_recv()
    img_proj = proj_ref[...]
    grad = block_ref[0] + block_in[0].astype(F32) + block_in[2].astype(F32)
    product = jnp.sum(img_proj * grad, axis=1, keepdims=True)
    grad = grad / img_len - img_proj * product / (img_len * img_len * img_len)
    grad_set[0] = grad.astype(BF16)
    grad_arrive = {}
    for r in (4, 6, 2, 1):
        grad_arrive[r] = send(grad_set.at[0], grad_set.at[r], along(r))

    gtz_arrive = {}
    for k in (1, 2, 3):
        gtx_arrive[k - 1].wait_recv()
        gtz_out[k] = (gtx_ref[k] + gtx_in[k].astype(F32)).astype(BF16)
        gtz_arrive[k] = send(gtz_out.at[k], gtz_in.at[k], along(2 * k))

    grad_norm = matmul_nt(grad_set[0], full_ref[...])
    img_hat = hat_ref[...]
    img_gain_sum = jnp.sum(grad_norm * img_hat, axis=0, keepdims=True)
    scaled = grad_norm * igain_ref[...]
    gif_ref[...] = img_inv * (
        scaled
        - jnp.mean(scaled, axis=1, keepdims=True)
        - img_hat * jnp.mean(scaled * img_hat, axis=1, keepdims=True)
    )

    for r in (2, 4, 6):
        grad_arrive[r].wait_recv()
        grad_arrive[r + 1] = send(grad_set.at[r], grad_set.at[r + 1], along(1))

    grad_proj = matmul(turned_in[0], grad_set[0])
    for r in (2, 4, 6):
        turned_arrive[r].wait_recv()
        grad_proj = grad_proj + matmul(turned_in[r], grad_set[r])

    gtx_arrive[3].wait_recv()
    grad = gtx_ref[0] + gtx_in[0].astype(F32)
    for k in (1, 2, 3):
        gtz_arrive[k].wait_recv()
        grad = grad + gtz_in[k].astype(F32)
    product = jnp.sum(txt_scaled * grad, axis=1, keepdims=True)
    grad = grad / txt_len - txt_scaled * product / (txt_len * txt_len * txt_len)
    txt_gain_sum = jnp.sum(grad * txt_hat, axis=0, keepdims=True)
    img_tiles = img_ref.shape[1] // 128
    txt_tiles = txt_ref.shape[1] // 128
    small_ref[...] = jnp.zeros_like(small_ref)
    for k in range(img_tiles):
        small_ref[k:k + 1, :] = img_gain_sum[:, k * 128:(k + 1) * 128]
    for k in range(txt_tiles):
        at = img_tiles + k
        small_ref[at:at + 1, :] = txt_gain_sum[:, k * 128:(k + 1) * 128]
    at = img_tiles + txt_tiles
    lanes = lax.broadcasted_iota(jnp.int32, (1, 128), 1)
    small_ref[at:at + 1, :] = jnp.where(
        lanes == 0, loss, jnp.where(lanes == 1, grad_scale, jnp.where(lanes == 2, grad_bias, 0.0))
    )
    small_arrive = [send(small_ref, small_in.at[b], across(r)) for r in (1, 2, 3)]

    scaled = grad * tgain_ref[...]
    gtf_ref[...] = txt_inv * (
        scaled
        - jnp.mean(scaled, axis=1, keepdims=True)
        - txt_hat * jnp.mean(scaled * txt_hat, axis=1, keepdims=True)
    )

    for r in (1, 3, 5, 7):
        turned_arrive[r].wait_recv()
        grad_arrive[r].wait_recv()
        grad_proj = grad_proj + matmul(turned_in[r], grad_set[r])
    gproj_ref[...] = grad_proj
    mine = pl.ds(pl.multiple_of(core * half, 16), half)
    other = pl.ds(pl.multiple_of((1 - core) * half, 16), half)
    gp_first = send(gproj_ref.at[other, :], gp_in, across(1))

    small_in[b] = small_ref[...]
    for copy in small_arrive:
        copy.wait_recv()
    mid_ref[...] = (small_in[0] + small_in[1]) + (small_in[2] + small_in[3])
    mid_arrive = [send(mid_ref, mid_in.at[f], along(r)) for r in range(1, 8)]
    mid_in[f] = mid_ref[...]

    gp_first.wait()
    gp_out[...] = (gproj_ref[mine, :] + gp_in[...]).astype(BF16)
    gp_step = send(gp_out, gp_far, across(2))

    for copy in mid_arrive:
        copy.wait_recv()
    sums = mid_in[0]
    for k in range(1, 8):
        sums = sums + mid_in[k]
    for k in range(img_tiles):
        gig_ref[k * 128:(k + 1) * 128] = sums[k]
    for k in range(txt_tiles):
        at = img_tiles + k
        gtg_ref[k * 128:(k + 1) * 128] = sums[at]
    at = img_tiles + txt_tiles
    loss_ref[...] = sums[at:at + 1, 0:1] / batch_total
    gscale_ref[...] = sums[at:at + 1, 1:2]
    gbias_ref[...] = sums[at:at + 1, 2:3]

    gp_step.wait_recv()
    gp_sum[...] = gp_out[...].astype(F32) + gp_far[...].astype(F32)
    gp_last = send(gp_sum, gp_end, across(1))
    gproj_ref[mine, :] = gp_sum[...]
    gp_last.wait_recv()
    gproj_ref[other, :] = gp_end[...]

    for copy in copies:
        if copy is not gp_first:
            copy.wait_send()


def fused_shards(img_feat, txt_feat, partner, projection, img_gain, txt_gain, log_scale, logit_bias):
    rows, width = img_feat.shape
    emb = txt_feat.shape[1]
    depth = projection.shape[0]
    batch_total = rows * lax.axis_size("blk") * lax.axis_size("fsdp")
    small_rows = -(-((width + emb) // 128 + 1) // 8) * 8
    scalar = jax.ShapeDtypeStruct((1, 1), F32)
    vmem = pltpu.VMEM
    outs = pl.pallas_call(
        functools.partial(kernel, batch_total),
        out_shape=(
            scalar,
            scalar,
            scalar,
            jax.ShapeDtypeStruct((depth, emb), F32),
            jax.ShapeDtypeStruct((width,), F32),
            jax.ShapeDtypeStruct((emb,), F32),
            jax.ShapeDtypeStruct((rows, width), F32),
            jax.ShapeDtypeStruct((rows, emb), F32),
        ),
        in_specs=[pl.BlockSpec(memory_space=vmem)] * 8,
        out_specs=tuple([pl.BlockSpec(memory_space=vmem)] * 8),
        scratch_shapes=[
            vmem((1, width), F32),
            vmem((1, emb), F32),
            vmem((width, emb), BF16),
            vmem((rows, width), BF16),
            vmem((rows, width), F32),
            vmem((width, rows), BF16),
            vmem((8, depth, rows), BF16),
            vmem((rows, emb), F32),
            vmem((8, rows, emb), BF16),
            vmem((4 * rows, emb), BF16),
            vmem((4 * rows, 8 * rows), BF16),
            vmem((8 * rows, 4 * rows), BF16),
            vmem((2, rows, emb), F32),
            vmem((3, rows, emb), BF16),
            vmem((3, rows, emb), BF16),
            vmem((4, rows, emb), F32),
            vmem((4, rows, emb), BF16),
            vmem((4, rows, emb), BF16),
            vmem((4, rows, emb), BF16),
            vmem((4, rows, emb), BF16),
            vmem((8, rows, emb), BF16),
            vmem((depth // 2, emb), F32),
            vmem((depth // 2, emb), BF16),
            vmem((depth // 2, emb), BF16),
            vmem((depth // 2, emb), F32),
            vmem((depth // 2, emb), F32),
            vmem((small_rows, 128), F32),
            vmem((4, small_rows, 128), F32),
            vmem((small_rows, 128), F32),
            vmem((8, small_rows, 128), F32),
            pltpu.SemaphoreType.DMA((80,)),
            pltpu.SemaphoreType.DMA((80,)),
        ],
        compiler_params=pltpu.CompilerParams(
            collective_id=0, has_side_effects=True, vmem_limit_bytes=48 * 1024 * 1024
        ),
    )(
        img_feat,
        txt_feat,
        partner.reshape(rows, 1),
        projection,
        img_gain,
        txt_gain,
        log_scale.reshape(1, 1),
        logit_bias.reshape(1, 1),
    )
    loss, grad_scale, grad_bias, grad_proj, img_sum, txt_sum, img_grad, txt_grad = outs
    return (
        loss.reshape(1),
        grad_scale.reshape(1),
        grad_bias.reshape(1),
        grad_proj,
        img_sum,
        txt_sum,
        img_grad,
        txt_grad,
    )


def solution(mesh):
    placed = (
        P(("blk", "fsdp"), None),
        P(("blk", "fsdp"), None),
        P(("blk", "fsdp")),
        P("fsdp", None),
        P(),
        P(),
        P(),
        P(),
    )
    fused = mesh.shape["blk"] == 4 and mesh.shape["fsdp"] == 8
    return jax.shard_map(
        fused_shards if fused else shards,
        mesh=mesh,
        in_specs=placed,
        out_specs=(
            P(),
            P(),
            P(),
            P("fsdp", None),
            P(),
            P(),
            P(("blk", "fsdp"), None),
            P(("blk", "fsdp"), None),
        ),
        check_vma=False,
    )
```
